256 devices in a mesh: bgrp: 4 (over x), fft: 64 (over z, y, core).
Axes of the slice: x: 4, y: 4, z: 8, core: 2. Of those that a mesh axis runs over, the one named last changes fastest.
Arguments:
- psi: float32 [8, 2, 8192, 128], P('bgrp', None, 'fft'), may hold values from -6 to 6
- potential: float32 [128, 128, 128], P('fft'), may hold values from -6 to 6
- basis: float32 [4, 2, 8192, 128], P(None, None, 'fft'), may hold values from -6 to 6
- stick_map: int32 [8192], P('fft'), may hold values from -1 to 16383, as said below
Outputs:
- hpsi: float32 [8, 2, 8192, 128], P('bgrp', None, 'fft')
- margin: float32 [2, 8, 4], replicated
The draws below stay inside these ranges and needn't reach their ends.
Inputs may be any that keep to these rules, and one draw needn't show every extreme that they name: `stick_map`: each slot holds -1 (empty) or a column x * 128 + y whose wrapped frequencies satisfy fx^2 + fy^2 <= 32^2; every such column appears in exactly one slot. The 128 slots of one index of fft hold its sticks first and then its empty slots; some index of fft has all of its slots filled.
All inputs are finite; a program needn't handle non-finite values.
Results may differ from the reference program's by a relative error of at most 0.000096.
Values sent between devices are 32-bit elements; how exact they have to be, the bound alone decides.
A program may use at most 128 MiB of HBM per device.

```python
import math
import jax
import jax.numpy as jnp
import numpy as np
from jax import lax

NG = 128
R = 32
BASIS = 4
BANDS = 8
SCAP = 128
STICKS = 8192
N_FFT = 64


def draw_stick_map(key, part):
    key = jax.random.fold_in(key, 7)
    offsets = np.arange(-R, R + 1)
    freq_x, freq_y = np.meshgrid(offsets, offsets, indexing='ij')
    inside = freq_x * freq_x + freq_y * freq_y <= R * R
    column_np = (freq_x[inside] % NG * NG + freq_y[inside] % NG).astype(np.int32)
    total_sticks = int(column_np.shape[0])
    columns = jnp.asarray(column_np)
    key_perm, key_heavy, key_weight, key_extra = jax.random.split(key, 4)
    shuffled = jax.random.permutation(key_perm, columns)
    heaviest = jax.random.randint(key_heavy, (), 0, N_FFT)
    devices = jnp.arange(N_FFT, dtype=jnp.int32)
    weights = jax.random.randint(key_weight, (N_FFT,), 2, 5)
    weights = jnp.where(devices == heaviest, 0, weights)
    remain = total_sticks - SCAP
    load_count = remain * weights // jnp.sum(weights)
    leftover = remain - jnp.sum(load_count)
    ranking = jax.random.permutation(key_extra, N_FFT - 1)
    others = jnp.clip(devices - (devices > heaviest).astype(jnp.int32), 0, N_FFT - 2)
    extra_one = jnp.where(devices == heaviest, 0, (ranking[others] < leftover).astype(jnp.int32))
    load_count = jnp.where(devices == heaviest, SCAP, load_count + extra_one)
    starts = jnp.cumsum(load_count) - load_count
    slot_index = jnp.arange(SCAP, dtype=jnp.int32)
    position = starts[:, None] + slot_index[None, :]
    filled = slot_index[None, :] < load_count[:, None]
    picked = shuffled[jnp.minimum(position, total_sticks - 1)]
    return jnp.where(filled, picked, -1).reshape(-1).astype(jnp.int32)


def level_of(rng, shape, cuts, low, top_value):
    gain = 1.0
    for axis_at, parts in cuts:
        heights = jax.random.uniform(jax.random.fold_in(jax.random.fold_in(rng, 6), axis_at), (parts,), jnp.float32, low / len(cuts), top_value / len(cuts))
        gain = gain * jnp.repeat(jnp.exp(heights), shape[axis_at] // parts).reshape((-1,) + (1,) * (len(shape) - 1 - axis_at))
    return gain


def noise(stream_key, extent, deviation, limit, shards=(), kind=jnp.bfloat16):
    factor_of = level_of(stream_key, extent, shards, -0.22, 0.18) if shards else 1.0
    drawn = jax.random.normal(stream_key, extent, jnp.float32) * deviation * factor_of
    return jnp.minimum(jnp.maximum(drawn, -limit), limit).astype(kind)


def setup_inputs(seed: int = 0) -> dict:
    key_list = jax.random.split(jax.random.key(seed), 5)
    psi = noise(key_list[0], (BANDS, 2, STICKS, NG), 1.0, 6.0, ((0, 4), (2, 64)), jnp.float32)
    potential = noise(key_list[1], (NG, NG, NG), 1.0, 6.0, ((0, 64),), jnp.float32)
    basis = noise(key_list[2], (BASIS, 2, STICKS, NG), 1.0, 6.0, ((2, 64),), jnp.float32)
    stick_map = draw_stick_map(jax.random.fold_in(key_list[4], 71), 0)
    return dict(psi=psi, potential=potential, basis=basis, stick_map=stick_map)


def wrapped(index):
    return jnp.where(index < NG // 2, index, index - NG)

def sphere_terms(columns, sample):
    occupied = columns >= 0
    safe_col = jnp.where(occupied, columns, 0)
    freq_x = wrapped(safe_col // NG)
    freq_y = wrapped(safe_col % NG)
    freq_z = wrapped(jnp.arange(NG, dtype=jnp.int32))
    square = (freq_x * freq_x + freq_y * freq_y)[:, None] + (freq_z * freq_z)[None, :]
    inside = occupied[:, None] & (square <= R * R)
    weight_in = inside.astype(sample.dtype)
    kinetic = weight_in * square.astype(sample.dtype) * (2.0 / (R * R))
    return (weight_in, kinetic)

def reference(psi, potential, basis, stick_map):
    weight_in, kinetic = sphere_terms(stick_map, psi)
    target = jnp.where(stick_map >= 0, stick_map, NG * NG).astype(jnp.int32)
    fetch = jnp.minimum(target, NG * NG - 1).astype(jnp.int32)

    def one_band(member):
        coef = lax.complex(member[0] * weight_in, member[1] * weight_in)
        zeros = jnp.zeros((NG, NG * NG), member.dtype)
        layout = lax.complex(zeros, zeros).at[:, target].set(coef.T, mode='drop')
        field = jnp.fft.ifftn(layout.reshape(NG, NG, NG), norm='ortho')
        image = jnp.fft.fftn(field * potential, norm='ortho').reshape(NG, NG * NG)
        values = image[:, fetch].T
        result = weight_in * values + kinetic * coef
        return jnp.stack([jnp.real(result), jnp.imag(result)])
    hpsi = lax.map(one_band, psi)
    scale = 1.0 / math.sqrt(4.0 * math.pi * R ** 3 / 3.0)
    flat_h = hpsi.reshape(hpsi.shape[0], 2, -1)
    flat_b = basis.reshape(basis.shape[0], 2, -1)
    high = lax.Precision.HIGHEST
    over_re = jnp.einsum('bn,kn->bk', flat_h[:, 0], flat_b[:, 0], precision=high) + jnp.einsum('bn,kn->bk', flat_h[:, 1], flat_b[:, 1], precision=high)
    over_im = jnp.einsum('bn,kn->bk', flat_h[:, 1], flat_b[:, 0], precision=high) - jnp.einsum('bn,kn->bk', flat_h[:, 0], flat_b[:, 1], precision=high)
    margin = jnp.stack([over_re, over_im]) * scale
    return (hpsi, margin)
```

```python
import functools
import math

import jax
import jax.numpy as jnp
import ml_dtypes
import numpy as np
from jax import lax
from jax.experimental import pallas as pl
from jax.experimental.pallas import tpu as pltpu
from jax.sharding import PartitionSpec as P

NG = 128
R = 32
NB = 2
NK = 4
ND = 64
NZ = 8
NYC = 8
XS = 72
SPOT = 80
F32 = jnp.float32
BF16 = jnp.bfloat16
MESH = pl.DeviceIdType.MESH


def split_np(table):
    high = table.astype(np.float32).astype(ml_dtypes.bfloat16)
    low = (table - high.astype(np.float64)).astype(np.float32).astype(ml_dtypes.bfloat16)
    return high, low


def phases(rows, cols):
    angle = 2.0 * np.pi / NG * (np.outer(rows, cols) % NG)
    return np.cos(angle) / math.sqrt(NG), np.sin(angle) / math.sqrt(NG)


def build_tables():
    index = np.arange(NG)
    slot = np.arange(ND)
    device = (slot % NZ) * NYC + slot // NZ
    z_rows = np.concatenate([2 * device, 2 * device + 1])
    cos, sin = phases(z_rows, index)
    wz = np.block([[cos, -sin], [sin, cos]])
    blocks = []
    for shifted in (0, 1):
        freq = index - 64 if shifted else index
        inner = (index >= 33) & (index <= 95)
        used = inner if shifted else ~inner
        cos, sin = phases(freq, index)
        cos, sin = cos * used[:, None], sin * used[:, None]
        blocks.append(np.block([[cos, sin], [-sin, cos]]))
    wy = np.concatenate(blocks, axis=1)
    freq = np.zeros(XS)
    freq[:32] = np.arange(32)
    freq[32:64] = -np.arange(32)
    freq[32] = -R
    freq[64] = R
    cos, sin = phases(index, freq)
    cos[:, 65:] = 0.0
    sin[:, 65:] = 0.0
    wx = np.block([[cos, -sin], [sin, cos]])
    tables = []
    for table, side in ((wz, 1), (wy, 0), (wx, 1), (wx.T, 1), (wy.T, 0), (wz.T, 1)):
        high, low = split_np(table)
        tables.append(np.concatenate([high, high, low], axis=side))
    pad = np.zeros((2 * NG, 512 - 6 * XS), ml_dtypes.bfloat16)
    tables[2] = np.concatenate([tables[2], pad], axis=1)
    return tables


TABLES = build_tables()


def split(value):
    high = value.astype(BF16)
    low = (value - high.astype(F32)).astype(BF16)
    return high, low


def dot(left, right, transposed=False):
    dims = (((1,), (1 if transposed else 0,)), ((), ()))
    return lax.dot_general(left, right, dims, preferred_element_type=F32)


def triple(value, axis):
    high, low = split(value)
    return jnp.concatenate([high, low, high], axis=axis)


def frequencies(col):
    cx = col >> 7
    cy = col & 127
    fx = jnp.where(cx < 64, cx, cx - NG)
    return fx, cy


def packed(col):
    fx, cy = frequencies(col)
    row = jnp.abs(fx) & 31
    lane = jnp.where(fx < 0, (cy + 64) & 127, cy)
    lane = jnp.where(fx == R, SPOT, lane)
    lane = lane + (row >> 4) * NG
    row = jnp.where(col < 0, -1, row & 15)
    return row, lane


def kernel(
    psi_h, pot_h, basis_h, stick_h, wz_h, wy_h, wx_h, wxb_h, wyb_h, wzb_h,
    hpsi_h, margin,
    psi, pot, basis, stick, wz, wy, wx, wxb, wyb, wzb,
    weight, kinetic, send, recv, back, home, cols, nhot, acc, lref, hout,
    tile1, tile2, m1, m2,
    load_sem, out_sem, own_sem, col_send, col_recv, fwd_send, fwd_recv,
    back_send, back_recv, mar_send, mar_recv,
):
    g = lax.axis_index("bgrp")
    me = lax.axis_index("fft")
    myz = me // NYC
    myyc = me % NYC
    myy = myyc // 2
    mycore = myyc % 2
    myslot = myyc * NZ + myz

    barrier = pltpu.get_barrier_semaphore()

    def greet(k, carry):
        peer = (me + k) % ND
        pl.semaphore_signal(barrier, inc=1, device_id=(g, peer), device_id_type=MESH)
        return carry

    lax.fori_loop(1, ND, greet, 0)

    def greet_far(k, carry):
        other = (g + 1 + k // 4) % 4
        peer = myz * NYC + (k % 4) * 2 + mycore
        pl.semaphore_signal(barrier, inc=1, device_id=(other, peer), device_id_type=MESH)
        return carry

    lax.fori_loop(0, 12, greet_far, 0)

    loads = []
    pairs = (
        (stick_h, stick), (psi_h, psi), (wz_h, wz), (wy_h, wy), (wx_h, wx), (pot_h, pot),
        (wxb_h, wxb), (wyb_h, wyb), (wzb_h, wzb), (basis_h, basis),
    )
    for k, (source, target) in enumerate(pairs):
        copy = pltpu.make_async_copy(source, target, load_sem.at[k])
        copy.start()
        loads.append(copy)
    loads[0].wait()
    col = stick[...]
    cols[myslot] = col
    fx, cy = frequencies(col)
    fy = jnp.where(cy < 64, cy, cy - NG)
    square = jnp.where(col < 0, 1 << 20, fx * fx + fy * fy).astype(F32)
    lanes = lax.broadcasted_iota(jnp.int32, (NG, NG), 1)
    fz = jnp.where(lanes < 64, lanes, lanes - NG)
    total = jnp.broadcast_to(square, (NG, NG)).T + (fz * fz).astype(F32)
    inside = total <= float(R * R)
    weight[...] = jnp.where(inside, 1.0, 0.0)
    kinetic[...] = jnp.where(inside, total * (2.0 / (R * R)), 0.0)

    pl.semaphore_wait(barrier, ND - 1 + 12)

    for k in range(1, NZ):
        peer = ((myz + k) % NZ) * NYC + myyc
        pltpu.make_async_remote_copy(
            src_ref=cols.at[myslot], dst_ref=cols.at[myslot],
            send_sem=col_send.at[0], recv_sem=col_recv.at[0],
            device_id=(g, peer), device_id_type=MESH,
        ).start()

    loads[1].wait()
    rows = []
    for b in range(NB):
        parts = []
        for c in range(2):
            coef = psi[b, c] * weight[...]
            psi[b, c] = coef
            parts.append(coef)
        rows.append(triple(jnp.concatenate(parts, axis=1), 1))
    loads[2].wait()
    space = dot(wz[...], jnp.concatenate(rows, axis=0), True)
    for c in range(2):
        for p in range(2):
            for b in range(NB):
                at = (c * 2 + p) * ND
                send[pl.ds(c * 4 + b * 2 + p, ND, stride=8), :] = space[
                    at : at + ND, b * NG : (b + 1) * NG
                ]

    some = cols.at[pl.ds(0, NZ - 1)]
    pltpu.make_async_copy(some, some, col_recv.at[0]).wait()
    mine = cols.at[pl.ds(myyc * NZ, NZ)]
    for k in range(1, NYC):
        peer = myz * NYC + (myyc + k) % NYC
        pltpu.make_async_remote_copy(
            src_ref=mine, dst_ref=mine,
            send_sem=col_send.at[1], recv_sem=col_recv.at[1],
            device_id=(g, peer), device_id_type=MESH,
        ).start()

    def block_at(slot):
        return pl.ds(pl.multiple_of(slot * 8, 8), 8)

    def transfer(source, target, z, yc, send_sem, recv_sem):
        pltpu.make_async_remote_copy(
            src_ref=source.at[block_at(yc * NZ + z)], dst_ref=target.at[block_at(myslot)],
            send_sem=send_sem, recv_sem=recv_sem,
            device_id=(g, z * NYC + yc), device_id_type=MESH,
        ).start()

    order = (4, 3, 5, 2, 6, 1, 7, 0)
    own = pltpu.make_async_copy(send.at[block_at(myslot)], recv.at[block_at(myslot)], own_sem.at[0])
    own.start()
    for k in order[:-1]:
        transfer(send, recv, (myz + k) % NZ, myyc, fwd_send, fwd_recv.at[myyc])

    def send_group(a, carry):
        yc = (myyc + a) % NYC
        for k in order:
            transfer(send, recv, (myz + k) % NZ, yc, fwd_send, fwd_recv.at[myyc])
        return carry

    lax.fori_loop(1, NYC, send_group, 0)

    most = cols.at[pl.ds(0, ND - NZ)]
    pltpu.make_async_copy(most, most, col_recv.at[1]).wait()

    def hot_group(yc):
        for q in range(NZ):
            _, lane = packed(cols[yc * NZ + q])
            hit = lax.broadcasted_iota(jnp.int32, (2 * NG, NG), 0) == lane
            at = pl.ds(pl.multiple_of((yc * NZ + q) * NG, NG), NG)
            nhot[:, at] = jnp.where(hit, 1.0, 0.0).astype(BF16)

    def place_group(yc):
        pieces = []
        for q in range(NZ):
            row, _ = packed(cols[yc * NZ + q])
            value = recv[block_at(yc * NZ + q), :]
            high = value.astype(BF16).astype(F32)
            low = value - high
            stack = [jnp.where(row == k, high, 0.0) for k in range(16)]
            stack += [jnp.where(row == k, low, 0.0) for k in range(16)]
            pieces.append(jnp.concatenate(stack, axis=0).astype(BF16))
        at = pl.ds(pl.multiple_of(yc * NZ * NG, NZ * NG), NZ * NG)
        acc[...] += dot(jnp.concatenate(pieces, axis=1), nhot[:, at], True)

    acc[...] = jnp.zeros_like(acc)
    hot_group(myyc)
    own.wait()
    seven = recv.at[pl.ds(0, 8 * (NZ - 1))]
    pltpu.make_async_copy(seven, seven, fwd_recv.at[myyc]).wait()
    place_group(myyc)

    def receive_group(a, carry):
        yc = (myyc + NYC - a) % NYC
        hot_group(yc)
        eight = recv.at[pl.ds(0, 8 * NZ)]
        pltpu.make_async_copy(eight, eight, fwd_recv.at[yc]).wait()
        place_group(yc)
        return carry

    lax.fori_loop(1, NYC, receive_group, 0)

    for h in range(2):
        half = slice(h * NG, (h + 1) * NG)
        lref[half, :] = acc[0:NG, half] + acc[NG : 2 * NG, half]
    spot = (lax.broadcasted_iota(jnp.int32, (8, NG), 0) == 0) & (
        lax.broadcasted_iota(jnp.int32, (8, NG), 1) == SPOT
    )
    factor = 1.0 / math.sqrt(NG)
    planes = []
    extra = {}
    for bp in range(4):
        parts = []
        for c in range(2):
            j = c * 4 + bp
            blocks = [lref[pl.ds(h * NG + j, 16, stride=8), :] for h in range(2)]
            first = blocks[0][0:8]
            single = jnp.sum(jnp.where(spot, first, 0.0), axis=1, keepdims=True) * factor
            extra[bp, c] = jnp.broadcast_to(single, (8, NG))
            first = jnp.where(spot, 0.0, first)
            parts.append(jnp.concatenate([first, blocks[0][8:16], blocks[1]], axis=0))
        planes.append(jnp.concatenate(parts, axis=1))
    loads[3].wait()
    along_y = dot(triple(jnp.concatenate(planes, axis=0), 1), wy[...])
    columns = []
    for bp in range(4):
        parts = []
        for c in range(2):
            for t in range(2):
                at = (t * 2 + c) * NG
                parts.append(along_y[bp * 32 : (bp + 1) * 32, at : at + NG])
            parts.append(extra[bp, c])
        columns.append(jnp.concatenate(parts, axis=0))
    high, low = split(jnp.concatenate(columns, axis=1))
    empty = jnp.zeros((512 - 6 * XS, 4 * NG), BF16)
    loads[4].wait()
    field = dot(wx[...], jnp.concatenate([high, low, high, empty], axis=0))
    loads[5].wait()
    both = jnp.concatenate([pot[0], pot[1], pot[0], pot[1]], axis=1)
    product = field * jnp.concatenate([both, both], axis=0)
    loads[6].wait()
    along_x = dot(wxb[...], triple(product, 0))
    planes = []
    for bp in range(4):
        parts = []
        for t in range(2):
            for c in range(2):
                at = c * XS + t * 32
                parts.append(along_x[at : at + 32, bp * NG : (bp + 1) * NG])
        planes.append(jnp.concatenate(parts, axis=1))
    loads[7].wait()
    image = dot(triple(jnp.concatenate(planes, axis=0), 1), wyb[...])
    for bp in range(4):
        for c in range(2):
            j = c * 4 + bp
            at = c * XS + 64
            tail = along_x[at : at + 8, bp * NG : (bp + 1) * NG]
            single = jnp.sum(tail, axis=1, keepdims=True) * factor
            part = image[bp * 32 : (bp + 1) * 32, c * NG : (c + 1) * NG]
            first = jnp.where(spot, single, part[0:8])
            lref[pl.ds(j, 16, stride=8), :] = jnp.concatenate([first, part[8:16]], axis=0)
            lref[pl.ds(NG + j, 16, stride=8), :] = part[16:32]
    high, low = split(jnp.concatenate([lref[0:NG, :], lref[NG : 2 * NG, :]], axis=1))
    acc_left = jnp.concatenate([high, low], axis=0)

    def fetch_group(yc):
        for q in range(0, NZ, 2):
            at = pl.ds(pl.multiple_of((yc * NZ + q) * NG, 2 * NG), 2 * NG)
            found = dot(acc_left, nhot[:, at])
            for w in range(2):
                slot = yc * NZ + q + w
                row, _ = packed(cols[slot])
                here = found[:, w * NG : (w + 1) * NG]
                total = jnp.zeros((8, NG), F32)
                for k in range(16):
                    both = here[k * 8 : k * 8 + 8] + here[NG + k * 8 : NG + k * 8 + 8]
                    total = total + jnp.where(row == k, both, 0.0)
                back[block_at(slot), :] = total

    def return_group(a, carry):
        yc = (myyc + a) % NYC
        fetch_group(yc)
        for k in order:
            transfer(back, home, (myz + k) % NZ, yc, back_send, back_recv)
        return carry

    lax.fori_loop(1, NYC, return_group, 0)
    fetch_group(myyc)
    for k in order[:-1]:
        transfer(back, home, (myz + k) % NZ, myyc, back_send, back_recv)
    own_back = pltpu.make_async_copy(
        back.at[block_at(myslot)], home.at[block_at(myslot)], own_sem.at[1]
    )
    own_back.start()
    loads[8].wait()
    loads[9].wait()
    own_back.wait()
    rest = home.at[pl.ds(0, 8 * (ND - 1))]
    pltpu.make_async_copy(rest, rest, back_recv).wait()

    sides = []
    for b in range(NB):
        parts = []
        for c in range(2):
            for p in range(2):
                parts.append(home[pl.ds(c * 4 + b * 2 + p, ND, stride=8), :])
        sides.append(jnp.concatenate(parts, axis=0))
    values = dot(wzb[...], triple(jnp.concatenate(sides, axis=1), 0))
    for b in range(NB):
        for c in range(2):
            turned = values[c * NG : (c + 1) * NG, b * NG : (b + 1) * NG].T
            hout[b, c] = weight[...] * turned + kinetic[...] * psi[b, c]
    result = pltpu.make_async_copy(hout, hpsi_h, out_sem)
    result.start()

    sums = []
    for b in range(NB):
        for c in range(2):
            for k in range(NK):
                if c == 0:
                    terms = hout[b, 0] * basis[k, 0] + hout[b, 1] * basis[k, 1]
                else:
                    terms = hout[b, 1] * basis[k, 0] - hout[b, 0] * basis[k, 1]
                sums.append(jnp.sum(terms, axis=0, keepdims=True))
    table = jnp.sum(jnp.concatenate(sums, axis=0), axis=1, keepdims=True)
    table = table * (1.0 / math.sqrt(4.0 * math.pi * R**3 / 3.0))
    tile_row = lax.broadcasted_iota(jnp.int32, (8, NG), 0)
    tile_lane = lax.broadcasted_iota(jnp.int32, (8, NG), 1)
    tile = jnp.zeros((8, NG), F32)
    for b in range(NB):
        for k in range(8):
            hit = (tile_row == g * NB + b) & (tile_lane == k)
            at = b * 8 + k
            tile = jnp.where(hit, table[at : at + 1, :], tile)

    def exchange(tile_ref, slots, slot, peers, which):
        for peer in peers:
            pltpu.make_async_remote_copy(
                src_ref=tile_ref, dst_ref=slots.at[block_at(slot)],
                send_sem=mar_send.at[which], recv_sem=mar_recv.at[which],
                device_id=peer, device_id_type=MESH,
            ).start()
        slots[block_at(slot), :] = tile_ref[...]
        part = slots.at[pl.ds(0, 8 * 15)]
        pltpu.make_async_copy(part, part, mar_recv.at[which]).wait()
        total = slots[0:8, :]
        for k in range(1, 16):
            total = total + slots[k * 8 : k * 8 + 8, :]
        return total

    tile1[...] = tile
    peers = []
    for k in range(1, 16):
        at = (myz * 2 + mycore + k) % 16
        peers.append((g, (at // 2) * NYC + myy * 2 + at % 2))
    tile2[...] = exchange(tile1, m1, myz * 2 + mycore, peers, 0)
    peers = []
    for k in range(1, 16):
        at = (g * 4 + myy + k) % 16
        peers.append((at // 4, myz * NYC + (at % 4) * 2 + mycore))
    final = exchange(tile2, m2, g * 4 + myy, peers, 1)
    margin[0] = final[:, 0:NK]
    margin[1] = final[:, NK : 2 * NK]

    pltpu.make_async_copy(some, some, col_send.at[0]).wait()
    pltpu.make_async_copy(most, most, col_send.at[1]).wait()
    pltpu.make_async_copy(rest, rest, fwd_send).wait()
    pltpu.make_async_copy(rest, rest, back_send).wait()
    part = m1.at[pl.ds(0, 8 * 15)]
    pltpu.make_async_copy(part, part, mar_send.at[0]).wait()
    pltpu.make_async_copy(part, part, mar_send.at[1]).wait()
    result.wait()


def body(psi, potential, basis, stick_map):
    shapes = [
        (psi.shape, F32), (potential.shape, F32), (basis.shape, F32), ((1, NG), jnp.int32),
    ]
    scratch = [pltpu.VMEM(shape, kind) for shape, kind in shapes]
    scratch += [pltpu.VMEM(table.shape, BF16) for table in TABLES]
    scratch += [
        pltpu.VMEM((NG, NG), F32),
        pltpu.VMEM((NG, NG), F32),
        pltpu.VMEM((ND * 8, NG), F32),
        pltpu.VMEM((ND * 8, NG), F32),
        pltpu.VMEM((ND * 8, NG), F32),
        pltpu.VMEM((ND * 8, NG), F32),
        pltpu.VMEM((ND, 1, NG), jnp.int32),
        pltpu.VMEM((2 * NG, ND * NG), BF16),
        pltpu.VMEM((2 * NG, 2 * NG), F32),
        pltpu.VMEM((2 * NG, NG), F32),
        pltpu.VMEM(psi.shape, F32),
        pltpu.VMEM((8, NG), F32),
        pltpu.VMEM((8, NG), F32),
        pltpu.VMEM((8 * 16, NG), F32),
        pltpu.VMEM((8 * 16, NG), F32),
        pltpu.SemaphoreType.DMA((10,)),
        pltpu.SemaphoreType.DMA,
        pltpu.SemaphoreType.DMA((2,)),
        pltpu.SemaphoreType.DMA((2,)),
        pltpu.SemaphoreType.DMA((2,)),
        pltpu.SemaphoreType.DMA,
        pltpu.SemaphoreType.DMA((NYC,)),
        pltpu.SemaphoreType.DMA,
        pltpu.SemaphoreType.DMA,
        pltpu.SemaphoreType.DMA((2,)),
        pltpu.SemaphoreType.DMA((2,)),
    ]
    hpsi, margin = pl.pallas_call(
        kernel,
        out_shape=(
            jax.ShapeDtypeStruct(psi.shape, F32),
            jax.ShapeDtypeStruct((2, 4 * NB, NK), F32),
        ),
        in_specs=[pl.BlockSpec(memory_space=pl.ANY)] * (4 + len(TABLES)),
        out_specs=(
            pl.BlockSpec(memory_space=pl.ANY),
            pl.BlockSpec(memory_space=pltpu.VMEM),
        ),
        scratch_shapes=scratch,
        compiler_params=pltpu.CompilerParams(
            collective_id=0, has_side_effects=True, vmem_limit_bytes=40 * 1024 * 1024
        ),
        cost_estimate=pl.CostEstimate(
            flops=20_000_000_000, bytes_accessed=6_000_000, transcendentals=0
        ),
    )(psi, potential, basis, stick_map.reshape(1, NG), *[jnp.asarray(t) for t in TABLES])
    return hpsi, margin


def solution(mesh):
    placed = (
        P("bgrp", None, "fft", None),
        P("fft", None, None),
        P(None, None, "fft", None),
        P("fft"),
    )
    return jax.shard_map(
        body,
        mesh=mesh,
        in_specs=placed,
        out_specs=(P("bgrp", None, "fft", None), P()),
        check_vma=False,
    )
```

```python
import functools
import math

import jax
import jax.numpy as jnp
import ml_dtypes
import numpy as np
from jax import lax
from jax.experimental import pallas as pl
from jax.experimental.pallas import tpu as pltpu
from jax.sharding import PartitionSpec as P

NG = 128
R = 32
NB = 2
NK = 4
ND = 64
NZ = 8
NYC = 8
XS = 72
SPOT = 80
VMEM_BYTES = 64 * 1024 * 1024
F32 = jnp.float32
BF16 = jnp.bfloat16
MESH = pl.DeviceIdType.MESH


def split_np(table):
    high = table.astype(np.float32).astype(ml_dtypes.bfloat16)
    low = (table - high.astype(np.float64)).astype(np.float32).astype(ml_dtypes.bfloat16)
    return high, low


def phases(rows, cols):
    angle = 2.0 * np.pi / NG * (np.outer(rows, cols) % NG)
    return np.cos(angle) / math.sqrt(NG), np.sin(angle) / math.sqrt(NG)


def build_tables():
    index = np.arange(NG)
    slot = np.arange(ND)
    device = (slot % NZ) * NYC + slot // NZ
    z_rows = np.concatenate([2 * device, 2 * device + 1])
    cos, sin = phases(z_rows, index)
    wz = np.block([[cos, -sin], [sin, cos]])
    blocks = []
    for shifted in (0, 1):
        freq = index - 64 if shifted else index
        inner = (index >= 33) & (index <= 95)
        used = inner if shifted else ~inner
        cos, sin = phases(freq, index)
        cos, sin = cos * used[:, None], sin * used[:, None]
        blocks.append(np.block([[cos, sin], [-sin, cos]]))
    wy = np.concatenate(blocks, axis=1)
    freq = np.zeros(XS)
    freq[:32] = np.arange(32)
    freq[32:64] = -np.arange(32)
    freq[32] = -R
    freq[64] = R
    cos, sin = phases(index, freq)
    cos[:, 65:] = 0.0
    sin[:, 65:] = 0.0
    wx = np.block([[cos, -sin], [sin, cos]])
    tables = []
    for table, side in ((wz, 1), (wy, 0), (wx, 1), (wx.T, 1), (wy.T, 0), (wz.T, 1)):
        high, low = split_np(table)
        tables.append(np.concatenate([high, high, low], axis=side))
    pad = np.zeros((2 * NG, 512 - 6 * XS), ml_dtypes.bfloat16)
    tables[2] = np.concatenate([tables[2], pad], axis=1)
    return tables


TABLES = build_tables()


def hops(dz, dy, dc):
    return min(dz, NZ - dz) + min(dy, 4 - dy) + 0.3 * dc


STEPS = sorted(
    ((dz, dy, dc) for dz in range(NZ) for dy in range(4) for dc in range(2)),
    key=lambda step: -hops(*step),
)[:-1]
FIRST = [step for step in STEPS if step[1] == 0]
SECOND = sorted(
    ((dx, dy) for dx in range(4) for dy in range(4)),
    key=lambda step: -(min(step[0], 4 - step[0]) + min(step[1], 4 - step[1])),
)[:-1]
FAR_Z = (4, 3, 5, 2, 6, 1, 7, 0)


def split(value):
    high = value.astype(BF16)
    low = (value - high.astype(F32)).astype(BF16)
    return high, low


def dot(left, right, transposed=False):
    dims = (((1,), (1 if transposed else 0,)), ((), ()))
    return lax.dot_general(left, right, dims, preferred_element_type=F32)


def triple(value, axis):
    high, low = split(value)
    return jnp.concatenate([high, low, high], axis=axis)


def frequencies(col):
    cx = col >> 7
    cy = col & 127
    fx = jnp.where(cx < 64, cx, cx - NG)
    return fx, cy


def packed(col):
    fx, cy = frequencies(col)
    row = jnp.abs(fx) & 31
    lane = jnp.where(fx < 0, (cy + 64) & 127, cy)
    lane = jnp.where(fx == R, SPOT, lane)
    lane = lane + (row >> 4) * NG
    row = jnp.where(col < 0, -1, row & 15)
    return row, lane


def kernel(
    psi_h, pot_h, basis_h, stick_h, wz_h, wy_h, wx_h, wxb_h, wyb_h, wzb_h,
    hpsi_h, margin,
    psi, pot, basis, stick, wz, wy, wx, wxb, wyb, wzb,
    weight, kinetic, send, recv, back, home, cols, nhot, acc, lref, hout, trial, local,
    tile1, tile2, m1, m2,
    load_sem, out_sem, own_sem, col_send, col_recv, fwd_send, fwd_recv,
    back_send, back_recv, mar_send, mar_recv,
):
    g = lax.axis_index("bgrp")
    me = lax.axis_index("fft")
    myz = me // NYC
    myyc = me % NYC
    myy = myyc // 2
    mycore = myyc % 2
    myslot = myyc * NZ + myz

    zs = [(myz + k) % NZ for k in range(NZ)]
    ys = [(myy + k) % 4 for k in range(4)]
    cores = [mycore, 1 - mycore]
    groups = [(g + k) % 4 for k in range(4)]

    loads = []
    pairs = (
        (stick_h, stick), (psi_h, psi), (wz_h, wz), (wy_h, wy), (wx_h, wx), (pot_h, pot),
        (wxb_h, wxb), (wyb_h, wyb), (wzb_h, wzb), (basis_h, basis),
    )
    for k, (source, target) in enumerate(pairs):
        loads.append(pltpu.make_async_copy(source, target, load_sem.at[k]))
    for k in range(3):
        loads[k].start()

    barrier = pltpu.get_barrier_semaphore()
    for dz, dy, dc in STEPS:
        peer = zs[dz] * NYC + ys[dy] * 2 + cores[dc]
        pl.semaphore_signal(barrier, inc=1, device_id=(g, peer), device_id_type=MESH)
    for dx, dy in SECOND:
        if dx:
            peer = myz * NYC + ys[dy] * 2 + mycore
            pl.semaphore_signal(
                barrier, inc=1, device_id=(groups[dx], peer), device_id_type=MESH
            )
    for k in (9, 3, 4, 5, 6, 7, 8):
        loads[k].start()

    loads[0].wait()
    col = stick[...]
    cols[me] = col
    fx, cy = frequencies(col)
    fy = jnp.where(cy < 64, cy, cy - NG)
    square = jnp.where(col < 0, 1 << 20, fx * fx + fy * fy).astype(F32)
    lanes = lax.broadcasted_iota(jnp.int32, (NG, NG), 1)
    fz = jnp.where(lanes < 64, lanes, lanes - NG)
    total = jnp.broadcast_to(square, (NG, NG)).T + (fz * fz).astype(F32)
    inside = total <= float(R * R)
    weight[...] = jnp.where(inside, 1.0, 0.0)
    kinetic[...] = jnp.where(inside, total * (2.0 / (R * R)), 0.0)

    def along_z(vectors):
        rows = [triple(jnp.concatenate(parts, axis=1), 1) for parts in vectors]
        return dot(wz[...], jnp.concatenate(rows, axis=0), True)

    loads[1].wait()
    for b in range(NB):
        for c in range(2):
            psi[b, c] = psi[b, c] * weight[...]
    loads[2].wait()
    space = along_z([(psi[b, 0], psi[b, 1]) for b in range(NB)])
    for c in range(2):
        for p in range(2):
            for b in range(NB):
                at = (c * 2 + p) * ND
                send[pl.ds(c * 4 + b * 2 + p, ND, stride=8), :] = space[
                    at : at + ND, b * NG : (b + 1) * NG
                ]

    pl.semaphore_wait(barrier, ND - 1 + 12)

    for dy in range(4):
        for dc in range(2):
            if dy + dc:
                pltpu.make_async_remote_copy(
                    src_ref=cols.at[me], dst_ref=cols.at[me],
                    send_sem=col_send.at[0], recv_sem=col_recv.at[0],
                    device_id=(g, myz * NYC + ys[dy] * 2 + cores[dc]), device_id_type=MESH,
                ).start()

    def block_at(slot):
        return pl.ds(pl.multiple_of(slot * 8, 8), 8)

    def transfer(source, target, z, yc, send_sem, recv_sem):
        pltpu.make_async_remote_copy(
            src_ref=source.at[block_at(yc * NZ + z)], dst_ref=target.at[block_at(myslot)],
            send_sem=send_sem, recv_sem=recv_sem,
            device_id=(g, z * NYC + yc), device_id_type=MESH,
        ).start()

    for dz, dy, dc in STEPS:
        transfer(send, recv, zs[dz], ys[dy] * 2 + cores[dc], fwd_send, fwd_recv.at[myyc])
    own = pltpu.make_async_copy(send.at[block_at(myslot)], recv.at[block_at(myslot)], own_sem.at[0])
    own.start()

    some = cols.at[pl.ds(0, NYC - 1)]
    pltpu.make_async_copy(some, some, col_recv.at[0]).wait()
    mine = cols.at[pl.ds(myz * NYC, NYC)]
    for k in FAR_Z[:-1]:
        pltpu.make_async_remote_copy(
            src_ref=mine, dst_ref=mine,
            send_sem=col_send.at[1], recv_sem=col_recv.at[1],
            device_id=(g, zs[k] * NYC + myyc), device_id_type=MESH,
        ).start()

    def products(vectors, trials):
        sums = []
        for v_re, v_im in vectors:
            for c in range(2):
                for b_re, b_im in trials:
                    if c == 0:
                        terms = v_re * b_re + v_im * b_im
                    else:
                        terms = v_im * b_re - v_re * b_im
                    sums.append(jnp.sum(terms, axis=0, keepdims=True))
        return jnp.concatenate(sums, axis=0)

    loads[9].wait()
    for k in range(NK):
        for c in range(2):
            basis[k, c] = basis[k, c] * weight[...]
    trial[...] = along_z([(basis[k, 0], basis[k, 1]) for k in range(NK)])
    kinetic_part = [
        (kinetic[...] * psi[b, 0], kinetic[...] * psi[b, 1]) for b in range(NB)
    ]
    local[...] = products(kinetic_part, [(basis[k, 0], basis[k, 1]) for k in range(NK)])

    most = cols.at[pl.ds(0, ND - NZ)]
    pltpu.make_async_copy(most, most, col_recv.at[1]).wait()

    def hot_group(yc):
        for q in range(NZ):
            _, lane = packed(cols[q * NYC + yc])
            hit = lax.broadcasted_iota(jnp.int32, (2 * NG, NG), 0) == lane
            at = pl.ds(pl.multiple_of((yc * NZ + q) * NG, NG), NG)
            nhot[:, at] = jnp.where(hit, 1.0, 0.0).astype(BF16)

    def place_group(yc):
        pieces = []
        for q in range(NZ):
            row, _ = packed(cols[q * NYC + yc])
            value = recv[block_at(yc * NZ + q), :]
            high = value.astype(BF16).astype(F32)
            low = value - high
            stack = [jnp.where(row == k, high, 0.0) for k in range(16)]
            stack += [jnp.where(row == k, low, 0.0) for k in range(16)]
            pieces.append(jnp.concatenate(stack, axis=0).astype(BF16))
        at = pl.ds(pl.multiple_of(yc * NZ * NG, NZ * NG), NZ * NG)
        acc[...] += dot(jnp.concatenate(pieces, axis=1), nhot[:, at], True)

    acc[...] = jnp.zeros_like(acc)
    hot_group(myyc)
    own.wait()
    seven = recv.at[pl.ds(0, 8 * (NZ - 1))]
    pltpu.make_async_copy(seven, seven, fwd_recv.at[myyc]).wait()
    place_group(myyc)

    def receive_group(a, carry):
        yc = (myyc + NYC - a) % NYC
        hot_group(yc)
        eight = recv.at[pl.ds(0, 8 * NZ)]
        pltpu.make_async_copy(eight, eight, fwd_recv.at[yc]).wait()
        place_group(yc)
        return carry

    lax.fori_loop(1, NYC, receive_group, 0)

    for h in range(2):
        half = slice(h * NG, (h + 1) * NG)
        lref[half, :] = acc[0:NG, half] + acc[NG : 2 * NG, half]
    spot = (lax.broadcasted_iota(jnp.int32, (8, NG), 0) == 0) & (
        lax.broadcasted_iota(jnp.int32, (8, NG), 1) == SPOT
    )
    factor = 1.0 / math.sqrt(NG)
    planes = []
    extra = {}
    for bp in range(4):
        parts = []
        for c in range(2):
            j = c * 4 + bp
            blocks = [lref[pl.ds(h * NG + j, 16, stride=8), :] for h in range(2)]
            first = blocks[0][0:8]
            single = jnp.sum(jnp.where(spot, first, 0.0), axis=1, keepdims=True) * factor
            extra[bp, c] = jnp.broadcast_to(single, (8, NG))
            first = jnp.where(spot, 0.0, first)
            parts.append(jnp.concatenate([first, blocks[0][8:16], blocks[1]], axis=0))
        planes.append(jnp.concatenate(parts, axis=1))
    loads[3].wait()
    along_y = dot(triple(jnp.concatenate(planes, axis=0), 1), wy[...])
    columns = []
    for bp in range(4):
        parts = []
        for c in range(2):
            for t in range(2):
                at = (t * 2 + c) * NG
                parts.append(along_y[bp * 32 : (bp + 1) * 32, at : at + NG])
            parts.append(extra[bp, c])
        columns.append(jnp.concatenate(parts, axis=0))
    high, low = split(jnp.concatenate(columns, axis=1))
    empty = jnp.zeros((512 - 6 * XS, 4 * NG), BF16)
    loads[4].wait()
    field = dot(wx[...], jnp.concatenate([high, low, high, empty], axis=0))
    loads[5].wait()
    both = jnp.concatenate([pot[0], pot[1], pot[0], pot[1]], axis=1)
    product = field * jnp.concatenate([both, both], axis=0)
    loads[6].wait()
    along_x = dot(wxb[...], triple(product, 0))
    planes = []
    for bp in range(4):
        parts = []
        for t in range(2):
            for c in range(2):
                at = c * XS + t * 32
                parts.append(along_x[at : at + 32, bp * NG : (bp + 1) * NG])
        planes.append(jnp.concatenate(parts, axis=1))
    loads[7].wait()
    image = dot(triple(jnp.concatenate(planes, axis=0), 1), wyb[...])
    for bp in range(4):
        for c in range(2):
            j = c * 4 + bp
            at = c * XS + 64
            tail = along_x[at : at + 8, bp * NG : (bp + 1) * NG]
            single = jnp.sum(tail, axis=1, keepdims=True) * factor
            part = image[bp * 32 : (bp + 1) * 32, c * NG : (c + 1) * NG]
            first = jnp.where(spot, single, part[0:8])
            lref[pl.ds(j, 16, stride=8), :] = jnp.concatenate([first, part[8:16]], axis=0)
            lref[pl.ds(NG + j, 16, stride=8), :] = part[16:32]
    high, low = split(jnp.concatenate([lref[0:NG, :], lref[NG : 2 * NG, :]], axis=1))
    acc_left = jnp.concatenate([high, low], axis=0)

    def fetch_group(yc):
        for q in range(0, NZ, 2):
            at = pl.ds(pl.multiple_of((yc * NZ + q) * NG, 2 * NG), 2 * NG)
            found = dot(acc_left, nhot[:, at])
            for w in range(2):
                slot = yc * NZ + q + w
                row, _ = packed(cols[(q + w) * NYC + yc])
                here = found[:, w * NG : (w + 1) * NG]
                total = jnp.zeros((8, NG), F32)
                for k in range(16):
                    both = here[k * 8 : k * 8 + 8] + here[NG + k * 8 : NG + k * 8 + 8]
                    total = total + jnp.where(row == k, both, 0.0)
                back[block_at(slot), :] = total

    def return_group(i, carry):
        far = i // 2
        dy = (2 + 3 * far + 3 * (far * (far - 1) // 2)) % 4
        yc = ((myy + dy) % 4) * 2 + (mycore + 1 + i) % 2
        fetch_group(yc)
        for k in FAR_Z:
            transfer(back, home, zs[k], yc, back_send, back_recv)
        return carry

    lax.fori_loop(0, NYC - 1, return_group, 0)
    fetch_group(myyc)
    for k in FAR_Z[:-1]:
        transfer(back, home, zs[k], myyc, back_send, back_recv)
    own_back = pltpu.make_async_copy(
        back.at[block_at(myslot)], home.at[block_at(myslot)], own_sem.at[1]
    )
    own_back.start()
    loads[8].wait()
    own_back.wait()
    rest = home.at[pl.ds(0, 8 * (ND - 1))]
    pltpu.make_async_copy(rest, rest, back_recv).wait()

    sides = []
    for b in range(NB):
        parts = []
        for c in range(2):
            for p in range(2):
                parts.append(home[pl.ds(c * 4 + b * 2 + p, ND, stride=8), :])
        sides.append(jnp.concatenate(parts, axis=0))
    table = local[...] + products(
        [(side[0:NG], side[NG : 2 * NG]) for side in sides],
        [
            (trial[0:NG, k * NG : (k + 1) * NG], trial[NG : 2 * NG, k * NG : (k + 1) * NG])
            for k in range(NK)
        ],
    )
    table = jnp.sum(table, axis=1, keepdims=True)
    table = table * (1.0 / math.sqrt(4.0 * math.pi * R**3 / 3.0))
    tile_row = lax.broadcasted_iota(jnp.int32, (8, NG), 0)
    tile_lane = lax.broadcasted_iota(jnp.int32, (8, NG), 1)
    tile = jnp.zeros((8, NG), F32)
    for b in range(NB):
        for k in range(8):
            hit = (tile_lane == g * NB + b) & (tile_row == k)
            at = b * 8 + k
            tile = jnp.where(hit, table[at : at + 1, :], tile)

    def spread(tile_ref, slots, slot, peers, which):
        for peer in peers:
            pltpu.make_async_remote_copy(
                src_ref=tile_ref, dst_ref=slots.at[block_at(slot)],
                send_sem=mar_send.at[which], recv_sem=mar_recv.at[which],
                device_id=peer, device_id_type=MESH,
            ).start()
        slots[block_at(slot), :] = tile_ref[...]

    def gathered(slots, which):
        part = slots.at[pl.ds(0, 8 * 15)]
        pltpu.make_async_copy(part, part, mar_recv.at[which]).wait()
        total = slots[0:8, :]
        for k in range(1, 16):
            total = total + slots[k * 8 : k * 8 + 8, :]
        return total

    tile1[...] = tile
    peers = [(g, zs[dz] * NYC + myy * 2 + cores[dc]) for dz, _, dc in FIRST]
    spread(tile1, m1, myz * 2 + mycore, peers, 0)

    values = dot(wzb[...], triple(jnp.concatenate(sides, axis=1), 0))
    for b in range(NB):
        for c in range(2):
            turned = values[c * NG : (c + 1) * NG, b * NG : (b + 1) * NG].T
            hout[b, c] = weight[...] * turned + kinetic[...] * psi[b, c]
    result = pltpu.make_async_copy(hout, hpsi_h, out_sem)
    result.start()

    tile2[...] = gathered(m1, 0)
    peers = [(groups[dx], myz * NYC + ys[dy] * 2 + mycore) for dx, dy in SECOND]
    spread(tile2, m2, g * 4 + myy, peers, 1)
    final = gathered(m2, 1)
    margin[0] = final[0:NK, 0 : 4 * NB]
    margin[1] = final[NK : 2 * NK, 0 : 4 * NB]

    pltpu.make_async_copy(some, some, col_send.at[0]).wait()
    pltpu.make_async_copy(most, most, col_send.at[1]).wait()
    pltpu.make_async_copy(rest, rest, fwd_send).wait()
    pltpu.make_async_copy(rest, rest, back_send).wait()
    part = m1.at[pl.ds(0, 8 * 15)]
    pltpu.make_async_copy(part, part, mar_send.at[0]).wait()
    pltpu.make_async_copy(part, part, mar_send.at[1]).wait()
    result.wait()


def body(psi, potential, basis, stick_map):
    shapes = [
        (psi.shape, F32), (potential.shape, F32), (basis.shape, F32), ((1, NG), jnp.int32),
    ]
    scratch = [pltpu.VMEM(shape, kind) for shape, kind in shapes]
    scratch += [pltpu.VMEM(table.shape, BF16) for table in TABLES]
    scratch += [
        pltpu.VMEM((NG, NG), F32),
        pltpu.VMEM((NG, NG), F32),
        pltpu.VMEM((ND * 8, NG), F32),
        pltpu.VMEM((ND * 8, NG), F32),
        pltpu.VMEM((ND * 8, NG), F32),
        pltpu.VMEM((ND * 8, NG), F32),
        pltpu.VMEM((ND, 1, NG), jnp.int32),
        pltpu.VMEM((2 * NG, ND * NG), BF16),
        pltpu.VMEM((2 * NG, 2 * NG), F32),
        pltpu.VMEM((2 * NG, NG), F32),
        pltpu.VMEM(psi.shape, F32),
        pltpu.VMEM((2 * NG, NK * NG), F32),
        pltpu.VMEM((16, NG), F32),
        pltpu.VMEM((8, NG), F32),
        pltpu.VMEM((8, NG), F32),
        pltpu.VMEM((8 * 16, NG), F32),
        pltpu.VMEM((8 * 16, NG), F32),
        pltpu.SemaphoreType.DMA((10,)),
        pltpu.SemaphoreType.DMA,
        pltpu.SemaphoreType.DMA((2,)),
        pltpu.SemaphoreType.DMA((2,)),
        pltpu.SemaphoreType.DMA((2,)),
        pltpu.SemaphoreType.DMA,
        pltpu.SemaphoreType.DMA((NYC,)),
        pltpu.SemaphoreType.DMA,
        pltpu.SemaphoreType.DMA,
        pltpu.SemaphoreType.DMA((2,)),
        pltpu.SemaphoreType.DMA((2,)),
    ]
    hpsi, margin = pl.pallas_call(
        kernel,
        out_shape=(
            jax.ShapeDtypeStruct(psi.shape, F32),
            jax.ShapeDtypeStruct((2, NK, 4 * NB), F32),
        ),
        in_specs=[pl.BlockSpec(memory_space=pl.ANY)] * (4 + len(TABLES)),
        out_specs=(
            pl.BlockSpec(memory_space=pl.ANY),
            pl.BlockSpec(memory_space=pltpu.VMEM),
        ),
        scratch_shapes=scratch,
        compiler_params=pltpu.CompilerParams(
            collective_id=0, has_side_effects=True, vmem_limit_bytes=VMEM_BYTES
        ),
        cost_estimate=pl.CostEstimate(
            flops=20_000_000_000, bytes_accessed=6_000_000, transcendentals=0
        ),
    )(psi, potential, basis, stick_map.reshape(1, NG), *[jnp.asarray(t) for t in TABLES])
    return hpsi, margin.transpose(0, 2, 1)


def solution(mesh):
    placed = (
        P("bgrp", None, "fft", None),
        P("fft", None, None),
        P(None, None, "fft", None),
        P("fft"),
    )
    return jax.shard_map(
        body,
        mesh=mesh,
        in_specs=placed,
        out_specs=(P("bgrp", None, "fft", None), P()),
        check_vma=False,
    )
```

```python
import functools
import math

import jax
import jax.numpy as jnp
import ml_dtypes
import numpy as np
from jax import lax
from jax.experimental import pallas as pl
from jax.experimental.pallas import tpu as pltpu
from jax.sharding import PartitionSpec as P

NG = 128
R = 32
NB = 2
NK = 4
ND = 64
NZ = 8
NYC = 8
XS = 72
SPOT = 80
VMEM_BYTES = 62 * 1024 * 1024
F32 = jnp.float32
BF16 = jnp.bfloat16
MESH = pl.DeviceIdType.MESH


def split_np(table):
    high = table.astype(np.float32).astype(ml_dtypes.bfloat16)
    low = (table - high.astype(np.float64)).astype(np.float32).astype(ml_dtypes.bfloat16)
    return high, low


def phases(rows, cols):
    angle = 2.0 * np.pi / NG * (np.outer(rows, cols) % NG)
    return np.cos(angle) / math.sqrt(NG), np.sin(angle) / math.sqrt(NG)


def build_tables():
    index = np.arange(NG)
    slot = np.arange(ND)
    device = (slot % NZ) * NYC + slot // NZ
    z_rows = np.concatenate([2 * device, 2 * device + 1])
    cos, sin = phases(z_rows, index)
    wz = np.block([[cos, -sin], [sin, cos]])
    blocks = []
    for shifted in (0, 1):
        freq = index - 64 if shifted else index
        inner = (index >= 33) & (index <= 95)
        used = inner if shifted else ~inner
        cos, sin = phases(freq, index)
        cos, sin = cos * used[:, None], sin * used[:, None]
        blocks.append(np.block([[cos, sin], [-sin, cos]]))
    wy = np.concatenate(blocks, axis=1)
    freq = np.zeros(XS)
    freq[:32] = np.arange(32)
    freq[32:64] = -np.arange(32)
    freq[32] = -R
    freq[64] = R
    cos, sin = phases(index, freq)
    cos[:, 65:] = 0.0
    sin[:, 65:] = 0.0
    wx = np.block([[cos, -sin], [sin, cos]])
    tables = []
    for table, side in ((wz, 1), (wy, 0), (wx, 1), (wx.T, 1), (wy.T, 0), (wz.T, 1)):
        high, low = split_np(table)
        tables.append(np.concatenate([high, high, low], axis=side))
    pad = np.zeros((2 * NG, 512 - 6 * XS), ml_dtypes.bfloat16)
    tables[2] = np.concatenate([tables[2], pad], axis=1)
    return tables


TABLES = build_tables()


def hops(dz, dy, dc):
    return min(dz, NZ - dz) + min(dy, 4 - dy) + 0.3 * dc


STEPS = sorted(
    ((dz, dy, dc) for dz in range(NZ) for dy in range(4) for dc in range(2)),
    key=lambda step: -hops(*step),
)[:-1]
FIRST = [step for step in STEPS if step[1] == 0]
SECOND = sorted(
    ((dx, dy) for dx in range(4) for dy in range(4)),
    key=lambda step: -(min(step[0], 4 - step[0]) + min(step[1], 4 - step[1])),
)[:-1]
FAR_Z = (4, 3, 5, 2, 6, 1, 7, 0)


def split(value):
    high = value.astype(BF16)
    low = (value - high.astype(F32)).astype(BF16)
    return high, low


def dot(left, right, transposed=False):
    dims = (((1,), (1 if transposed else 0,)), ((), ()))
    return lax.dot_general(left, right, dims, preferred_element_type=F32)


def triple(value, axis):
    high, low = split(value)
    return jnp.concatenate([high, low, high], axis=axis)


def frequencies(col):
    cx = col >> 7
    cy = col & 127
    fx = jnp.where(cx < 64, cx, cx - NG)
    return fx, cy


def packed(col):
    fx, cy = frequencies(col)
    row = jnp.abs(fx) & 31
    lane = jnp.where(fx < 0, (cy + 64) & 127, cy)
    lane = jnp.where(fx == R, SPOT, lane)
    lane = lane + (row >> 4) * NG
    row = jnp.where(col < 0, -1, row & 15)
    return row, lane


def kernel(
    psi_h, pot_h, basis_h, stick_h, wz_h, wy_h, wx_h, wxb_h, wyb_h, wzb_h,
    hout, margin,
    psi, pot, basis, stick, wz, wy, wx, wxb, wyb, wzb,
    weight, kinetic, send, recv, back, home, nhot, acc, lref, trial, local, ramp,
    tile1, tile2, m1, m2,
    load_sem, own_sem, fwd_send, fwd_recv,
    back_send, back_recv, mar_send, mar_recv,
):
    g = lax.axis_index("bgrp")
    me = lax.axis_index("fft")
    myz = me // NYC
    myyc = me % NYC
    myy = myyc // 2
    mycore = myyc % 2
    myslot = myyc * NZ + myz

    zs = [(myz + k) % NZ for k in range(NZ)]
    ys = [(myy + k) % 4 for k in range(4)]
    cores = [mycore, 1 - mycore]
    groups = [(g + k) % 4 for k in range(4)]

    loads = []
    pairs = (
        (stick_h, stick), (psi_h, psi), (wz_h, wz), (wy_h, wy), (wx_h, wx), (pot_h, pot),
        (wxb_h, wxb), (wyb_h, wyb), (wzb_h, wzb), (basis_h, basis),
    )
    for k, (source, target) in enumerate(pairs):
        loads.append(pltpu.make_async_copy(source, target, load_sem.at[k]))
    for k in range(3):
        loads[k].start()

    barrier = pltpu.get_barrier_semaphore()
    for dz, dy, dc in STEPS:
        peer = zs[dz] * NYC + ys[dy] * 2 + cores[dc]
        pl.semaphore_signal(barrier, inc=1, device_id=(g, peer), device_id_type=MESH)
    for dx, dy in SECOND:
        if dx:
            peer = myz * NYC + ys[dy] * 2 + mycore
            pl.semaphore_signal(
                barrier, inc=1, device_id=(groups[dx], peer), device_id_type=MESH
            )
    for k in (9, 3, 4, 5, 6, 7, 8):
        loads[k].start()

    loads[0].wait()
    col = stick[...]
    fx, cy = frequencies(col)
    fy = jnp.where(cy < 64, cy, cy - NG)
    square = jnp.where(col < 0, 1 << 20, fx * fx + fy * fy).astype(F32)
    lanes = lax.broadcasted_iota(jnp.int32, (NG, NG), 1)
    fz = jnp.where(lanes < 64, lanes, lanes - NG)
    total = jnp.broadcast_to(square, (NG, NG)).T + (fz * fz).astype(F32)
    inside = total <= float(R * R)
    weight[...] = jnp.where(inside, 1.0, 0.0)
    kinetic[...] = jnp.where(inside, total * (2.0 / (R * R)), 0.0)

    def along_z(vectors):
        rows = [triple(jnp.concatenate(parts, axis=1), 1) for parts in vectors]
        return dot(wz[...], jnp.concatenate(rows, axis=0), True)

    loads[1].wait()
    for b in range(NB):
        for c in range(2):
            psi[b, c] = psi[b, c] * weight[...]
    loads[2].wait()
    space = along_z([(psi[b, 0], psi[b, 1]) for b in range(NB)])
    for c in range(2):
        for p in range(2):
            for b in range(NB):
                at = (c * 2 + p) * ND
                send[pl.ds(c * 4 + b * 2 + p, ND, stride=16), :] = space[
                    at : at + ND, b * NG : (b + 1) * NG
                ]

    send[pl.ds(8, ND, stride=16), :] = jnp.broadcast_to(col.astype(F32), (ND, NG))

    pl.semaphore_wait(barrier, ND - 1 + 12)

    def block_at(slot):
        return pl.ds(pl.multiple_of(slot * 8, 8), 8)

    def nine_at(slot):
        return pl.ds(pl.multiple_of(slot * 16, 16), 9)

    def transfer(source, target, place, z, yc, send_sem, recv_sem):
        pltpu.make_async_remote_copy(
            src_ref=source.at[place(yc * NZ + z)], dst_ref=target.at[place(myslot)],
            send_sem=send_sem, recv_sem=recv_sem,
            device_id=(g, z * NYC + yc), device_id_type=MESH,
        ).start()

    for dy in (0, 1, 3, 2):
        for dc in range(2):
            for k in FAR_Z:
                if dy + dc + k:
                    yc = ys[dy] * 2 + cores[dc]
                    transfer(send, recv, nine_at, zs[k], yc, fwd_send, fwd_recv.at[myyc])
    own = pltpu.make_async_copy(send.at[nine_at(myslot)], recv.at[nine_at(myslot)], own_sem.at[0])
    own.start()

    def products(vectors, trials):
        sums = []
        for v_re, v_im in vectors:
            for c in range(2):
                for b_re, b_im in trials:
                    if c == 0:
                        terms = v_re * b_re + v_im * b_im
                    else:
                        terms = v_im * b_re - v_re * b_im
                    sums.append(jnp.sum(terms, axis=0, keepdims=True))
        return jnp.concatenate(sums, axis=0)

    index = lax.broadcasted_iota(jnp.int32, (2 * NG, NG), 0)
    ramp[0 : 2 * NG, :] = index.astype(F32).astype(BF16)
    ramp[2 * NG : 3 * NG, :] = (index[0:NG] >> 3).astype(F32).astype(BF16)
    loads[9].wait()
    for k in range(NK):
        for c in range(2):
            basis[k, c] = basis[k, c] * weight[...]
    trial[...] = along_z([(basis[k, 0], basis[k, 1]) for k in range(NK)])
    kinetic_part = [
        (kinetic[...] * psi[b, 0], kinetic[...] * psi[b, 1]) for b in range(NB)
    ]
    local[...] = products(kinetic_part, [(basis[k, 0], basis[k, 1]) for k in range(NK)])

    one = jnp.ones((16, NG), BF16)
    zero = jnp.zeros((16, NG), BF16)

    def column(slot):
        return recv[pl.ds(slot * 16 + 8, 1), :].astype(jnp.int32)

    def landed(blocks, sem):
        some = recv.at[pl.ds(0, 9 * blocks)]
        pltpu.make_async_copy(some, some, sem).wait()

    def hot_group(yc):
        for q in range(NZ):
            _, lane = packed(column(yc * NZ + q))
            lane = jnp.broadcast_to(lane.astype(F32), (16, NG)).astype(BF16)
            at = pl.ds(pl.multiple_of((yc * NZ + q) * NG, NG), NG)
            for k in range(16):
                rows = pl.ds(k * 16, 16)
                nhot[rows, at] = jnp.where(ramp[rows, :] == lane, one, zero)

    def place_group(yc):
        pieces = []
        for q in range(NZ):
            row, _ = packed(column(yc * NZ + q))
            value = recv[pl.ds(pl.multiple_of((yc * NZ + q) * 16, 16), 8), :]
            row = jnp.broadcast_to(row.astype(F32), (16, NG)).astype(BF16)
            high, low = split(jnp.concatenate([value, value], axis=0))
            hits = [ramp[pl.ds(2 * NG + k * 16, 16), :] == row for k in range(8)]
            stack = [jnp.where(hit, part, zero) for part in (high, low) for hit in hits]
            pieces.append(jnp.concatenate(stack, axis=0))
        at = pl.ds(pl.multiple_of(yc * NZ * NG, NZ * NG), NZ * NG)
        acc[...] += dot(jnp.concatenate(pieces, axis=1), nhot[:, at], True)

    acc[...] = jnp.zeros_like(acc)
    own.wait()
    landed(NZ - 1, fwd_recv.at[myyc])
    hot_group(myyc)
    place_group(myyc)

    def receive_group(i, carry):
        far = i // 2
        dy = (3 * far + 3 * (far * (far - 1) // 2)) % 4
        yc = ((myy + dy) % 4) * 2 + (mycore + i) % 2
        landed(NZ, fwd_recv.at[yc])
        hot_group(yc)
        place_group(yc)
        return carry

    lax.fori_loop(1, NYC, receive_group, 0)

    for h in range(2):
        half = slice(h * NG, (h + 1) * NG)
        lref[half, :] = acc[0:NG, half] + acc[NG : 2 * NG, half]
    spot = (lax.broadcasted_iota(jnp.int32, (8, NG), 0) == 0) & (
        lax.broadcasted_iota(jnp.int32, (8, NG), 1) == SPOT
    )
    factor = 1.0 / math.sqrt(NG)
    planes = []
    extra = {}
    for bp in range(4):
        parts = []
        for c in range(2):
            j = c * 4 + bp
            blocks = [lref[pl.ds(h * NG + j, 16, stride=8), :] for h in range(2)]
            first = blocks[0][0:8]
            single = jnp.sum(jnp.where(spot, first, 0.0), axis=1, keepdims=True) * factor
            extra[bp, c] = jnp.broadcast_to(single, (8, NG))
            first = jnp.where(spot, 0.0, first)
            parts.append(jnp.concatenate([first, blocks[0][8:16], blocks[1]], axis=0))
        planes.append(jnp.concatenate(parts, axis=1))
    loads[3].wait()
    along_y = dot(triple(jnp.concatenate(planes, axis=0), 1), wy[...])
    columns = []
    for bp in range(4):
        parts = []
        for c in range(2):
            for t in range(2):
                at = (t * 2 + c) * NG
                parts.append(along_y[bp * 32 : (bp + 1) * 32, at : at + NG])
            parts.append(extra[bp, c])
        columns.append(jnp.concatenate(parts, axis=0))
    high, low = split(jnp.concatenate(columns, axis=1))
    empty = jnp.zeros((512 - 6 * XS, 4 * NG), BF16)
    loads[4].wait()
    field = dot(wx[...], jnp.concatenate([high, low, high, empty], axis=0))
    loads[5].wait()
    both = jnp.concatenate([pot[0], pot[1], pot[0], pot[1]], axis=1)
    product = field * jnp.concatenate([both, both], axis=0)
    loads[6].wait()
    along_x = dot(wxb[...], triple(product, 0))
    planes = []
    for bp in range(4):
        parts = []
        for t in range(2):
            for c in range(2):
                at = c * XS + t * 32
                parts.append(along_x[at : at + 32, bp * NG : (bp + 1) * NG])
        planes.append(jnp.concatenate(parts, axis=1))
    loads[7].wait()
    image = dot(triple(jnp.concatenate(planes, axis=0), 1), wyb[...])
    for bp in range(4):
        for c in range(2):
            j = c * 4 + bp
            at = c * XS + 64
            tail = along_x[at : at + 8, bp * NG : (bp + 1) * NG]
            single = jnp.sum(tail, axis=1, keepdims=True) * factor
            part = image[bp * 32 : (bp + 1) * 32, c * NG : (c + 1) * NG]
            first = jnp.where(spot, single, part[0:8])
            lref[pl.ds(j, 16, stride=8), :] = jnp.concatenate([first, part[8:16]], axis=0)
            lref[pl.ds(NG + j, 16, stride=8), :] = part[16:32]
    high, low = split(jnp.concatenate([lref[0:NG, :], lref[NG : 2 * NG, :]], axis=1))
    acc_left = jnp.concatenate([high, low], axis=0)

    def fetch_group(yc):
        for q in range(0, NZ, 2):
            at = pl.ds(pl.multiple_of((yc * NZ + q) * NG, 2 * NG), 2 * NG)
            found = dot(acc_left, nhot[:, at])
            for w in range(2):
                slot = yc * NZ + q + w
                row, _ = packed(column(slot))
                here = found[:, w * NG : (w + 1) * NG]
                total = jnp.zeros((8, NG), F32)
                for k in range(16):
                    both = here[k * 8 : k * 8 + 8] + here[NG + k * 8 : NG + k * 8 + 8]
                    total = total + jnp.where(row == k, both, 0.0)
                back[block_at(slot), :] = total

    def return_group(i, carry):
        far = i // 2
        dy = (2 + 3 * far + 3 * (far * (far - 1) // 2)) % 4
        yc = ((myy + dy) % 4) * 2 + (mycore + 1 + i) % 2
        fetch_group(yc)
        for k in FAR_Z:
            transfer(back, home, block_at, zs[k], yc, back_send, back_recv)
        return carry

    lax.fori_loop(0, NYC - 1, return_group, 0)
    fetch_group(myyc)
    for k in FAR_Z[:-1]:
        transfer(back, home, block_at, zs[k], myyc, back_send, back_recv)
    own_back = pltpu.make_async_copy(
        back.at[block_at(myslot)], home.at[block_at(myslot)], own_sem.at[1]
    )
    own_back.start()
    loads[8].wait()
    own_back.wait()
    rest = home.at[pl.ds(0, 8 * (ND - 1))]
    pltpu.make_async_copy(rest, rest, back_recv).wait()

    sides = []
    for b in range(NB):
        parts = []
        for c in range(2):
            for p in range(2):
                parts.append(home[pl.ds(c * 4 + b * 2 + p, ND, stride=8), :])
        sides.append(jnp.concatenate(parts, axis=0))
    table = local[...] + products(
        [(side[0:NG], side[NG : 2 * NG]) for side in sides],
        [
            (trial[0:NG, k * NG : (k + 1) * NG], trial[NG : 2 * NG, k * NG : (k + 1) * NG])
            for k in range(NK)
        ],
    )
    table = jnp.sum(table, axis=1, keepdims=True)
    table = table * (1.0 / math.sqrt(4.0 * math.pi * R**3 / 3.0))
    tile_row = lax.broadcasted_iota(jnp.int32, (8, NG), 0)
    tile_lane = lax.broadcasted_iota(jnp.int32, (8, NG), 1)
    tile = jnp.zeros((8, NG), F32)
    for b in range(NB):
        for k in range(8):
            hit = (tile_lane == g * NB + b) & (tile_row == k)
            at = b * 8 + k
            tile = jnp.where(hit, table[at : at + 1, :], tile)

    def spread(tile_ref, slots, slot, peers, which):
        for peer in peers:
            pltpu.make_async_remote_copy(
                src_ref=tile_ref, dst_ref=slots.at[block_at(slot)],
                send_sem=mar_send.at[which], recv_sem=mar_recv.at[which],
                device_id=peer, device_id_type=MESH,
            ).start()
        slots[block_at(slot), :] = tile_ref[...]

    def gathered(slots, which):
        part = slots.at[pl.ds(0, 8 * 15)]
        pltpu.make_async_copy(part, part, mar_recv.at[which]).wait()
        total = slots[0:8, :]
        for k in range(1, 16):
            total = total + slots[k * 8 : k * 8 + 8, :]
        return total

    tile1[...] = tile
    peers = [(g, zs[dz] * NYC + myy * 2 + cores[dc]) for dz, _, dc in FIRST]
    spread(tile1, m1, myz * 2 + mycore, peers, 0)

    values = dot(wzb[...], triple(jnp.concatenate(sides, axis=1), 0))
    for b in range(NB):
        for c in range(2):
            turned = values[c * NG : (c + 1) * NG, b * NG : (b + 1) * NG].T
            hout[b, c] = weight[...] * turned + kinetic[...] * psi[b, c]

    tile2[...] = gathered(m1, 0)
    peers = [(groups[dx], myz * NYC + ys[dy] * 2 + mycore) for dx, dy in SECOND]
    spread(tile2, m2, g * 4 + myy, peers, 1)
    final = gathered(m2, 1)
    margin[0] = final[0:NK, 0 : 4 * NB]
    margin[1] = final[NK : 2 * NK, 0 : 4 * NB]

    sent = recv.at[pl.ds(0, 9 * (ND - 1))]
    pltpu.make_async_copy(sent, sent, fwd_send).wait()
    pltpu.make_async_copy(rest, rest, back_send).wait()
    part = m1.at[pl.ds(0, 8 * 15)]
    pltpu.make_async_copy(part, part, mar_send.at[0]).wait()
    pltpu.make_async_copy(part, part, mar_send.at[1]).wait()


def body(psi, potential, basis, stick_map):
    shapes = [
        (psi.shape, F32), (potential.shape, F32), (basis.shape, F32), ((1, NG), jnp.int32),
    ]
    scratch = [pltpu.VMEM(shape, kind) for shape, kind in shapes]
    scratch += [pltpu.VMEM(table.shape, BF16) for table in TABLES]
    scratch += [
        pltpu.VMEM((NG, NG), F32),
        pltpu.VMEM((NG, NG), F32),
        pltpu.VMEM((ND * 16, NG), F32),
        pltpu.VMEM((ND * 16, NG), F32),
        pltpu.VMEM((ND * 8, NG), F32),
        pltpu.VMEM((ND * 8, NG), F32),
        pltpu.VMEM((2 * NG, ND * NG), BF16),
        pltpu.VMEM((2 * NG, 2 * NG), F32),
        pltpu.VMEM((2 * NG, NG), F32),
        pltpu.VMEM((2 * NG, NK * NG), F32),
        pltpu.VMEM((16, NG), F32),
        pltpu.VMEM((3 * NG, NG), BF16),
        pltpu.VMEM((8, NG), F32),
        pltpu.VMEM((8, NG), F32),
        pltpu.VMEM((8 * 16, NG), F32),
        pltpu.VMEM((8 * 16, NG), F32),
        pltpu.SemaphoreType.DMA((10,)),
        pltpu.SemaphoreType.DMA((2,)),
        pltpu.SemaphoreType.DMA,
        pltpu.SemaphoreType.DMA((NYC,)),
        pltpu.SemaphoreType.DMA,
        pltpu.SemaphoreType.DMA,
        pltpu.SemaphoreType.DMA((2,)),
        pltpu.SemaphoreType.DMA((2,)),
    ]
    hpsi, margin = pl.pallas_call(
        kernel,
        out_shape=(
            pltpu.VMEM(psi.shape, F32),
            pltpu.VMEM((2, NK, 4 * NB), F32),
        ),
        in_specs=[pl.BlockSpec(memory_space=pltpu.HBM)] * (4 + len(TABLES)),
        out_specs=(
            pl.BlockSpec(memory_space=pltpu.VMEM),
            pl.BlockSpec(memory_space=pltpu.VMEM),
        ),
        scratch_shapes=scratch,
        compiler_params=pltpu.CompilerParams(
            collective_id=0, has_side_effects=True, vmem_limit_bytes=VMEM_BYTES
        ),
        cost_estimate=pl.CostEstimate(
            flops=20_000_000_000, bytes_accessed=6_000_000, transcendentals=0
        ),
    )(psi, potential, basis, stick_map.reshape(1, NG), *[jnp.asarray(t) for t in TABLES])
    return hpsi, margin.transpose(0, 2, 1)


def solution(mesh):
    placed = (
        P("bgrp", None, "fft", None),
        P("fft", None, None),
        P(None, None, "fft", None),
        P("fft"),
    )
    return jax.shard_map(
        body,
        mesh=mesh,
        in_specs=placed,
        out_specs=(P("bgrp", None, "fft", None), P()),
        check_vma=False,
    )
```

```python
import functools
import math

import jax
import jax.numpy as jnp
import ml_dtypes
import numpy as np
from jax import lax
from jax.experimental import pallas as pl
from jax.experimental.pallas import tpu as pltpu
from jax.sharding import PartitionSpec as P

NG = 128
R = 32
NB = 2
NK = 4
ND = 64
NZ = 8
NYC = 8
XS = 72
SPOT = 80
VMEM_BYTES = 62 * 1024 * 1024
F32 = jnp.float32
BF16 = jnp.bfloat16
MESH = pl.DeviceIdType.MESH


def split_np(table):
    high = table.astype(np.float32).astype(ml_dtypes.bfloat16)
    low = (table - high.astype(np.float64)).astype(np.float32).astype(ml_dtypes.bfloat16)
    return high, low


def phases(rows, cols):
    angle = 2.0 * np.pi / NG * (np.outer(rows, cols) % NG)
    return np.cos(angle) / math.sqrt(NG), np.sin(angle) / math.sqrt(NG)


def build_tables():
    index = np.arange(NG)
    slot = np.arange(ND)
    device = (slot % NZ) * NYC + slot // NZ
    z_rows = np.concatenate([2 * device, 2 * device + 1])
    cos, sin = phases(z_rows, index)
    wz = np.block([[cos, -sin], [sin, cos]])
    blocks = []
    for shifted in (0, 1):
        freq = index - 64 if shifted else index
        inner = (index >= 33) & (index <= 95)
        used = inner if shifted else ~inner
        cos, sin = phases(freq, index)
        cos, sin = cos * used[:, None], sin * used[:, None]
        blocks.append(np.block([[cos, sin], [-sin, cos]]))
    wy = np.concatenate(blocks, axis=1)
    freq = np.zeros(XS)
    freq[:32] = np.arange(32)
    freq[32:64] = -np.arange(32)
    freq[32] = -R
    freq[64] = R
    cos, sin = phases(index, freq)
    cos[:, 65:] = 0.0
    sin[:, 65:] = 0.0
    wx = np.block([[cos, -sin], [sin, cos]])
    tables = []
    for table, side in ((wz, 1), (wy, 0), (wx, 1), (wx.T, 1), (wy.T, 0), (wz.T, 1)):
        high, low = split_np(table)
        tables.append(np.concatenate([high, high, low], axis=side))
    pad = np.zeros((2 * NG, 512 - 6 * XS), ml_dtypes.bfloat16)
    tables[2] = np.concatenate([tables[2], pad], axis=1)
    return tables


TABLES = build_tables()


def hops(dz, dy, dc):
    return min(dz, NZ - dz) + min(dy, 4 - dy) + 0.3 * dc


STEPS = sorted(
    ((dz, dy, dc) for dz in range(NZ) for dy in range(4) for dc in range(2)),
    key=lambda step: -hops(*step),
)[:-1]
SECOND = [(dx, dy) for dx in (2, 1, 3) for dy in (2, 1, 3, 0)]
FAR_Z = (4, 3, 5, 2, 6, 1, 7, 0)


def split(value):
    high = value.astype(BF16)
    low = (value - high.astype(F32)).astype(BF16)
    return high, low


def dot(left, right, transposed=False):
    dims = (((1,), (1 if transposed else 0,)), ((), ()))
    return lax.dot_general(left, right, dims, preferred_element_type=F32)


def triple(value, axis):
    high, low = split(value)
    return jnp.concatenate([high, low, high], axis=axis)


def frequencies(col):
    cx = col >> 7
    cy = col & 127
    fx = jnp.where(cx < 64, cx, cx - NG)
    return fx, cy


def packed(col):
    fx, cy = frequencies(col)
    row = jnp.abs(fx) & 31
    lane = jnp.where(fx < 0, (cy + 64) & 127, cy)
    lane = jnp.where(fx == R, SPOT, lane)
    lane = lane + (row >> 4) * NG
    row = jnp.where(col < 0, -1, row & 15)
    return row, lane


def kernel(
    psi_h, pot_h, basis_h, stick_h, wz_h, wy_h, wx_h, wxb_h, wyb_h, wzb_h,
    hout, margin,
    psi, pot, basis, stick, wz, wy, wx, wxb, wyb, wzb,
    weight, kinetic, send, recv, back, home, nhot, acc, lref, trial, local, ramp,
    tile1, tile2, chips,
    load_sem, own_sem, fwd_send, fwd_recv,
    back_send, back_recv, mar_send, mar_recv,
):
    g = lax.axis_index("bgrp")
    me = lax.axis_index("fft")
    myz = me // NYC
    myyc = me % NYC
    myy = myyc // 2
    mycore = myyc % 2
    myslot = myyc * NZ + myz

    zs = [(myz + k) % NZ for k in range(NZ)]
    ys = [(myy + k) % 4 for k in range(4)]
    cores = [mycore, 1 - mycore]
    groups = [(g + k) % 4 for k in range(4)]

    loads = []
    pairs = (
        (stick_h, stick), (psi_h, psi), (wz_h, wz), (wy_h, wy), (wx_h, wx), (pot_h, pot),
        (wxb_h, wxb), (wyb_h, wyb), (wzb_h, wzb), (basis_h, basis),
    )
    for k, (source, target) in enumerate(pairs):
        loads.append(pltpu.make_async_copy(source, target, load_sem.at[k]))
    for k in range(3):
        loads[k].start()

    barrier = pltpu.get_barrier_semaphore()
    for dz, dy, dc in STEPS:
        peer = zs[dz] * NYC + ys[dy] * 2 + cores[dc]
        pl.semaphore_signal(barrier, inc=1, device_id=(g, peer), device_id_type=MESH)
    for dx, dy in SECOND:
        peer = myz * NYC + ys[dy] * 2 + mycore
        pl.semaphore_signal(barrier, inc=1, device_id=(groups[dx], peer), device_id_type=MESH)
    for k in (9, 3, 4, 5, 6, 7, 8):
        loads[k].start()

    loads[0].wait()
    col = stick[...]
    fx, cy = frequencies(col)
    fy = jnp.where(cy < 64, cy, cy - NG)
    square = jnp.where(col < 0, 1 << 20, fx * fx + fy * fy).astype(F32)
    lanes = lax.broadcasted_iota(jnp.int32, (NG, NG), 1)
    fz = jnp.where(lanes < 64, lanes, lanes - NG)
    total = jnp.broadcast_to(square, (NG, NG)).T + (fz * fz).astype(F32)
    inside = total <= float(R * R)
    weight[...] = jnp.where(inside, 1.0, 0.0)
    kinetic[...] = jnp.where(inside, total * (2.0 / (R * R)), 0.0)

    def along_z(vectors):
        rows = [triple(jnp.concatenate(parts, axis=1), 1) for parts in vectors]
        return dot(wz[...], jnp.concatenate(rows, axis=0), True)

    loads[1].wait()
    for b in range(NB):
        for c in range(2):
            psi[b, c] = psi[b, c] * weight[...]
    loads[2].wait()
    space = along_z([(psi[b, 0], psi[b, 1]) for b in range(NB)])
    for c in range(2):
        for p in range(2):
            for b in range(NB):
                at = (c * 2 + p) * ND
                send[pl.ds(c * 4 + b * 2 + p, ND, stride=16), :] = space[
                    at : at + ND, b * NG : (b + 1) * NG
                ]

    send[pl.ds(8, ND, stride=16), :] = jnp.broadcast_to(col.astype(F32), (ND, NG))

    pl.semaphore_wait(barrier, ND - 1 + 12)

    def block_at(slot):
        return pl.ds(pl.multiple_of(slot * 8, 8), 8)

    def nine_at(slot):
        return pl.ds(pl.multiple_of(slot * 16, 16), 9)

    def transfer(source, target, place, z, yc, send_sem, recv_sem):
        pltpu.make_async_remote_copy(
            src_ref=source.at[place(yc * NZ + z)], dst_ref=target.at[place(myslot)],
            send_sem=send_sem, recv_sem=recv_sem,
            device_id=(g, z * NYC + yc), device_id_type=MESH,
        ).start()

    for dy in (0, 1, 3, 2):
        for dc in range(2):
            for k in FAR_Z:
                if dy + dc + k:
                    yc = ys[dy] * 2 + cores[dc]
                    transfer(send, recv, nine_at, zs[k], yc, fwd_send, fwd_recv.at[myyc])
    own = pltpu.make_async_copy(send.at[nine_at(myslot)], recv.at[nine_at(myslot)], own_sem.at[0])
    own.start()

    def products(vectors, trials):
        sums = []
        for v_re, v_im in vectors:
            for c in range(2):
                for b_re, b_im in trials:
                    if c == 0:
                        terms = v_re * b_re + v_im * b_im
                    else:
                        terms = v_im * b_re - v_re * b_im
                    sums.append(jnp.sum(terms, axis=0, keepdims=True))
        return jnp.concatenate(sums, axis=0)

    index = lax.broadcasted_iota(jnp.int32, (2 * NG, NG), 0)
    ramp[0 : 2 * NG, :] = index.astype(F32).astype(BF16)
    ramp[2 * NG : 3 * NG, :] = (index[0:NG] >> 3).astype(F32).astype(BF16)
    loads[9].wait()
    for k in range(NK):
        for c in range(2):
            basis[k, c] = basis[k, c] * weight[...]
    trial[...] = along_z([(basis[k, 0], basis[k, 1]) for k in range(NK)])
    kinetic_part = [
        (kinetic[...] * psi[b, 0], kinetic[...] * psi[b, 1]) for b in range(NB)
    ]
    local[...] = products(kinetic_part, [(basis[k, 0], basis[k, 1]) for k in range(NK)])

    one = jnp.ones((16, NG), BF16)
    zero = jnp.zeros((16, NG), BF16)

    def column(slot):
        return recv[pl.ds(slot * 16 + 8, 1), :].astype(jnp.int32)

    def landed(blocks, sem):
        some = recv.at[pl.ds(0, 9 * blocks)]
        pltpu.make_async_copy(some, some, sem).wait()

    def hot_group(yc):
        for q in range(NZ):
            _, lane = packed(column(yc * NZ + q))
            lane = jnp.broadcast_to(lane.astype(F32), (16, NG)).astype(BF16)
            at = pl.ds(pl.multiple_of((yc * NZ + q) * NG, NG), NG)
            for k in range(16):
                rows = pl.ds(k * 16, 16)
                nhot[rows, at] = jnp.where(ramp[rows, :] == lane, one, zero)

    def place_group(yc):
        pieces = []
        for q in range(NZ):
            row, _ = packed(column(yc * NZ + q))
            value = recv[pl.ds(pl.multiple_of((yc * NZ + q) * 16, 16), 8), :]
            row = jnp.broadcast_to(row.astype(F32), (16, NG)).astype(BF16)
            high, low = split(jnp.concatenate([value, value], axis=0))
            hits = [ramp[pl.ds(2 * NG + k * 16, 16), :] == row for k in range(8)]
            stack = [jnp.where(hit, part, zero) for part in (high, low) for hit in hits]
            pieces.append(jnp.concatenate(stack, axis=0))
        at = pl.ds(pl.multiple_of(yc * NZ * NG, NZ * NG), NZ * NG)
        acc[...] += dot(jnp.concatenate(pieces, axis=1), nhot[:, at], True)

    acc[...] = jnp.zeros_like(acc)
    own.wait()
    landed(NZ - 1, fwd_recv.at[myyc])
    hot_group(myyc)
    place_group(myyc)

    def receive_group(i, carry):
        far = i // 2
        dy = (3 * far + 3 * (far * (far - 1) // 2)) % 4
        yc = ((myy + dy) % 4) * 2 + (mycore + i) % 2
        landed(NZ, fwd_recv.at[yc])
        hot_group(yc)
        place_group(yc)
        return carry

    lax.fori_loop(1, NYC, receive_group, 0)

    for h in range(2):
        half = slice(h * NG, (h + 1) * NG)
        lref[half, :] = acc[0:NG, half] + acc[NG : 2 * NG, half]
    spot = (lax.broadcasted_iota(jnp.int32, (8, NG), 0) == 0) & (
        lax.broadcasted_iota(jnp.int32, (8, NG), 1) == SPOT
    )
    factor = 1.0 / math.sqrt(NG)
    planes = []
    extra = {}
    for bp in range(4):
        parts = []
        for c in range(2):
            j = c * 4 + bp
            blocks = [lref[pl.ds(h * NG + j, 16, stride=8), :] for h in range(2)]
            first = blocks[0][0:8]
            single = jnp.sum(jnp.where(spot, first, 0.0), axis=1, keepdims=True) * factor
            extra[bp, c] = jnp.broadcast_to(single, (8, NG))
            first = jnp.where(spot, 0.0, first)
            parts.append(jnp.concatenate([first, blocks[0][8:16], blocks[1]], axis=0))
        planes.append(jnp.concatenate(parts, axis=1))
    loads[3].wait()
    along_y = dot(triple(jnp.concatenate(planes, axis=0), 1), wy[...])
    columns = []
    for bp in range(4):
        parts = []
        for c in range(2):
            for t in range(2):
                at = (t * 2 + c) * NG
                parts.append(along_y[bp * 32 : (bp + 1) * 32, at : at + NG])
            parts.append(extra[bp, c])
        columns.append(jnp.concatenate(parts, axis=0))
    high, low = split(jnp.concatenate(columns, axis=1))
    empty = jnp.zeros((512 - 6 * XS, 4 * NG), BF16)
    loads[4].wait()
    field = dot(wx[...], jnp.concatenate([high, low, high, empty], axis=0))
    loads[5].wait()
    both = jnp.concatenate([pot[0], pot[1], pot[0], pot[1]], axis=1)
    product = field * jnp.concatenate([both, both], axis=0)
    loads[6].wait()
    along_x = dot(wxb[...], triple(product, 0))
    planes = []
    for bp in range(4):
        parts = []
        for t in range(2):
            for c in range(2):
                at = c * XS + t * 32
                parts.append(along_x[at : at + 32, bp * NG : (bp + 1) * NG])
        planes.append(jnp.concatenate(parts, axis=1))
    loads[7].wait()
    image = dot(triple(jnp.concatenate(planes, axis=0), 1), wyb[...])
    for bp in range(4):
        for c in range(2):
            j = c * 4 + bp
            at = c * XS + 64
            tail = along_x[at : at + 8, bp * NG : (bp + 1) * NG]
            single = jnp.sum(tail, axis=1, keepdims=True) * factor
            part = image[bp * 32 : (bp + 1) * 32, c * NG : (c + 1) * NG]
            first = jnp.where(spot, single, part[0:8])
            lref[pl.ds(j, 16, stride=8), :] = jnp.concatenate([first, part[8:16]], axis=0)
            lref[pl.ds(NG + j, 16, stride=8), :] = part[16:32]
    high, low = split(jnp.concatenate([lref[0:NG, :], lref[NG : 2 * NG, :]], axis=1))
    acc_left = jnp.concatenate([high, low], axis=0)

    def fetch_group(yc):
        for q in range(0, NZ, 2):
            at = pl.ds(pl.multiple_of((yc * NZ + q) * NG, 2 * NG), 2 * NG)
            found = dot(acc_left, nhot[:, at])
            for w in range(2):
                slot = yc * NZ + q + w
                row, _ = packed(column(slot))
                here = found[:, w * NG : (w + 1) * NG]
                total = jnp.zeros((8, NG), F32)
                for k in range(16):
                    both = here[k * 8 : k * 8 + 8] + here[NG + k * 8 : NG + k * 8 + 8]
                    total = total + jnp.where(row == k, both, 0.0)
                back[block_at(slot), :] = total

    def return_group(i, carry):
        far = i // 2
        dy = (2 + 3 * far + 3 * (far * (far - 1) // 2)) % 4
        yc = ((myy + dy) % 4) * 2 + (mycore + 1 + i) % 2
        fetch_group(yc)
        for k in FAR_Z:
            transfer(back, home, block_at, zs[k], yc, back_send, back_recv)
        return carry

    lax.fori_loop(0, NYC - 1, return_group, 0)
    fetch_group(myyc)
    for k in FAR_Z[:-1]:
        transfer(back, home, block_at, zs[k], myyc, back_send, back_recv)
    own_back = pltpu.make_async_copy(
        back.at[block_at(myslot)], home.at[block_at(myslot)], own_sem.at[1]
    )
    own_back.start()
    loads[8].wait()
    own_back.wait()
    rest = home.at[pl.ds(0, 8 * (ND - 1))]
    pltpu.make_async_copy(rest, rest, back_recv).wait()

    sides = []
    for b in range(NB):
        parts = []
        for c in range(2):
            for p in range(2):
                parts.append(home[pl.ds(c * 4 + b * 2 + p, ND, stride=8), :])
        sides.append(jnp.concatenate(parts, axis=0))
    table = local[...] + products(
        [(side[0:NG], side[NG : 2 * NG]) for side in sides],
        [
            (trial[0:NG, k * NG : (k + 1) * NG], trial[NG : 2 * NG, k * NG : (k + 1) * NG])
            for k in range(NK)
        ],
    )
    table = jnp.sum(table, axis=1, keepdims=True)
    table = table * (1.0 / math.sqrt(4.0 * math.pi * R**3 / 3.0))
    lane = lax.broadcasted_iota(jnp.int32, (1, NG), 1)
    entry = jnp.zeros((1, NG), F32)
    for k in range(16):
        entry = jnp.where(lane == k, table[k : k + 1, :], entry)
    tile1[...] = entry
    pair = pltpu.make_async_remote_copy(
        src_ref=tile1, dst_ref=tile2, send_sem=mar_send.at[0], recv_sem=mar_recv.at[0],
        device_id=(g, myz * NYC + myy * 2 + 1 - mycore), device_id_type=MESH,
    )
    pair.start()
    pair.wait()
    mychip = g * 32 + myz * 4 + myy
    chips[mychip] = entry + tile2[...]

    def tell(dx, z, dy):
        pltpu.make_async_remote_copy(
            src_ref=chips.at[mychip], dst_ref=chips.at[mychip],
            send_sem=mar_send.at[1], recv_sem=mar_recv.at[1],
            device_id=(groups[dx], z * NYC + ys[dy] * 2 + mycore), device_id_type=MESH,
        ).start()

    def tell_far(i, carry):
        z = (myz + 4 + ((i + 1) // 2) * (1 - 2 * (i % 2))) % NZ
        for dx in (2, 1, 3, 0):
            for dy in (2, 1, 3, 0):
                tell(dx, z, dy)
        return carry

    lax.fori_loop(0, NZ - 1, tell_far, 0)
    for dx in (2, 1, 3, 0):
        for dy in (2, 1, 3, 0):
            if dx + dy:
                tell(dx, myz, dy)

    values = dot(wzb[...], triple(jnp.concatenate(sides, axis=1), 0))
    for b in range(NB):
        for c in range(2):
            turned = values[c * NG : (c + 1) * NG, b * NG : (b + 1) * NG].T
            hout[b, c] = weight[...] * turned + kinetic[...] * psi[b, c]

    others = chips.at[pl.ds(0, 127)]
    pltpu.make_async_copy(others, others, mar_recv.at[1]).wait()
    row8 = lax.broadcasted_iota(jnp.int32, (8, NG), 0)
    lane8 = lax.broadcasted_iota(jnp.int32, (8, NG), 1)
    final = jnp.zeros((8, NG), F32)
    for group in range(4):
        total = chips[group * 32]
        for k in range(1, 32):
            total = total + chips[group * 32 + k]
        for b in range(NB):
            picked = jnp.where(lane8 == row8 + b * 8, total, 0.0)
            picked = jnp.sum(picked, axis=1, keepdims=True)
            final = jnp.where(lane8 == group * NB + b, picked, final)
    margin[0] = final[0:NK, 0 : 4 * NB]
    margin[1] = final[NK : 2 * NK, 0 : 4 * NB]

    sent = recv.at[pl.ds(0, 9 * (ND - 1))]
    pltpu.make_async_copy(sent, sent, fwd_send).wait()
    pltpu.make_async_copy(rest, rest, back_send).wait()
    pltpu.make_async_copy(others, others, mar_send.at[1]).wait()


def body(psi, potential, basis, stick_map):
    shapes = [
        (psi.shape, F32), (potential.shape, F32), (basis.shape, F32), ((1, NG), jnp.int32),
    ]
    scratch = [pltpu.VMEM(shape, kind) for shape, kind in shapes]
    scratch += [pltpu.VMEM(table.shape, BF16) for table in TABLES]
    scratch += [
        pltpu.VMEM((NG, NG), F32),
        pltpu.VMEM((NG, NG), F32),
        pltpu.VMEM((ND * 16, NG), F32),
        pltpu.VMEM((ND * 16, NG), F32),
        pltpu.VMEM((ND * 8, NG), F32),
        pltpu.VMEM((ND * 8, NG), F32),
        pltpu.VMEM((2 * NG, ND * NG), BF16),
        pltpu.VMEM((2 * NG, 2 * NG), F32),
        pltpu.VMEM((2 * NG, NG), F32),
        pltpu.VMEM((2 * NG, NK * NG), F32),
        pltpu.VMEM((16, NG), F32),
        pltpu.VMEM((3 * NG, NG), BF16),
        pltpu.VMEM((1, NG), F32),
        pltpu.VMEM((1, NG), F32),
        pltpu.VMEM((128, 1, NG), F32),
        pltpu.SemaphoreType.DMA((10,)),
        pltpu.SemaphoreType.DMA((2,)),
        pltpu.SemaphoreType.DMA,
        pltpu.SemaphoreType.DMA((NYC,)),
        pltpu.SemaphoreType.DMA,
        pltpu.SemaphoreType.DMA,
        pltpu.SemaphoreType.DMA((2,)),
        pltpu.SemaphoreType.DMA((2,)),
    ]
    hpsi, margin = pl.pallas_call(
        kernel,
        out_shape=(
            pltpu.VMEM(psi.shape, F32),
            pltpu.VMEM((2, NK, 4 * NB), F32),
        ),
        in_specs=[pl.BlockSpec(memory_space=pltpu.HBM)] * (4 + len(TABLES)),
        out_specs=(
            pl.BlockSpec(memory_space=pltpu.VMEM),
            pl.BlockSpec(memory_space=pltpu.VMEM),
        ),
        scratch_shapes=scratch,
        compiler_params=pltpu.CompilerParams(
            collective_id=0, has_side_effects=True, vmem_limit_bytes=VMEM_BYTES
        ),
        cost_estimate=pl.CostEstimate(
            flops=20_000_000_000, bytes_accessed=6_000_000, transcendentals=0
        ),
    )(psi, potential, basis, stick_map.reshape(1, NG), *[jnp.asarray(t) for t in TABLES])
    return hpsi, margin.transpose(0, 2, 1)


def solution(mesh):
    placed = (
        P("bgrp", None, "fft", None),
        P("fft", None, None),
        P(None, None, "fft", None),
        P("fft"),
    )
    return jax.shard_map(
        body,
        mesh=mesh,
        in_specs=placed,
        out_specs=(P("bgrp", None, "fft", None), P()),
        check_vma=False,
    )
```

```python
import functools
import math

import jax
import jax.numpy as jnp
import ml_dtypes
import numpy as np
from jax import lax
from jax.experimental import pallas as pl
from jax.experimental.pallas import tpu as pltpu
from jax.sharding import PartitionSpec as P

NG = 128
R = 32
NB = 2
NK = 4
ND = 64
NZ = 8
NYC = 8
XS = 72
SPOT = 80
VMEM_BYTES = 62 * 1024 * 1024
F32 = jnp.float32
BF16 = jnp.bfloat16
MESH = pl.DeviceIdType.MESH


def split_np(table):
    high = table.astype(np.float32).astype(ml_dtypes.bfloat16)
    low = (table - high.astype(np.float64)).astype(np.float32).astype(ml_dtypes.bfloat16)
    return high, low


def phases(rows, cols):
    angle = 2.0 * np.pi / NG * (np.outer(rows, cols) % NG)
    return np.cos(angle) / math.sqrt(NG), np.sin(angle) / math.sqrt(NG)


def build_tables():
    index = np.arange(NG)
    slot = np.arange(ND)
    device = (slot % NZ) * NYC + slot // NZ
    z_rows = np.concatenate([2 * device, 2 * device + 1])
    cos, sin = phases(z_rows, index)
    wz = np.block([[cos, -sin], [sin, cos]])
    blocks = []
    for shifted in (0, 1):
        freq = index - 64 if shifted else index
        inner = (index >= 33) & (index <= 95)
        used = inner if shifted else ~inner
        cos, sin = phases(freq, index)
        cos, sin = cos * used[:, None], sin * used[:, None]
        blocks.append(np.block([[cos, sin], [-sin, cos]]))
    wy = np.concatenate(blocks, axis=1)
    freq = np.zeros(XS)
    freq[:32] = np.arange(32)
    freq[32:64] = -np.arange(32)
    freq[32] = -R
    freq[64] = R
    cos, sin = phases(index, freq)
    cos[:, 65:] = 0.0
    sin[:, 65:] = 0.0
    wx = np.block([[cos, -sin], [sin, cos]])
    tables = []
    for table, side in ((wz, 1), (wy, 0), (wx, 1), (wx.T, 1), (wy.T, 0), (wz.T, 1)):
        high, low = split_np(table)
        tables.append(np.concatenate([high, high, low], axis=side))
    pad = np.zeros((2 * NG, 512 - 6 * XS), ml_dtypes.bfloat16)
    tables[2] = np.concatenate([tables[2], pad], axis=1)
    return tables


TABLES = build_tables()


def hops(dz, dy, dc):
    return min(dz, NZ - dz) + min(dy, 4 - dy) + 0.3 * dc


STEPS = sorted(
    ((dz, dy, dc) for dz in range(NZ) for dy in range(4) for dc in range(2)),
    key=lambda step: -hops(*step),
)[:-1]
SECOND = [(dx, dy) for dx in (2, 1, 3) for dy in (2, 1, 3, 0)]
FAR_Z = (4, 3, 5, 2, 6, 1, 7, 0)


def split(value):
    high = value.astype(BF16)
    low = (value - high.astype(F32)).astype(BF16)
    return high, low


def dot(left, right, transposed=False):
    dims = (((1,), (1 if transposed else 0,)), ((), ()))
    return lax.dot_general(left, right, dims, preferred_element_type=F32)


def triple(value, axis):
    high, low = split(value)
    return jnp.concatenate([high, low, high], axis=axis)


def frequencies(col):
    cx = col >> 7
    cy = col & 127
    fx = jnp.where(cx < 64, cx, cx - NG)
    return fx, cy


def packed(col):
    fx, cy = frequencies(col)
    row = jnp.abs(fx) & 31
    lane = jnp.where(fx < 0, (cy + 64) & 127, cy)
    lane = jnp.where(fx == R, SPOT, lane)
    lane = lane + (row >> 4) * NG
    row = jnp.where(col < 0, -1, row & 15)
    return row, lane


def kernel(
    psi_h, pot_h, basis_h, stick_h, wz_h, wy_h, wx_h, wxb_h, wyb_h, wzb_h,
    hout, margin,
    psi, pot, basis, stick, wz, wy, wx, wxb, wyb, wzb,
    weight, kinetic, send, recv, back, home, nhot, acc, lref, trial, local, ramp,
    tile1, tile2, chips,
    load_sem, own_sem, fwd_send, fwd_recv,
    back_send, back_recv, mar_send, mar_recv,
):
    g = lax.axis_index("bgrp")
    me = lax.axis_index("fft")
    myz = me // NYC
    myyc = me % NYC
    myy = myyc // 2
    mycore = myyc % 2
    myslot = myyc * NZ + myz

    zs = [(myz + k) % NZ for k in range(NZ)]
    ys = [(myy + k) % 4 for k in range(4)]
    cores = [mycore, 1 - mycore]
    groups = [(g + k) % 4 for k in range(4)]

    loads = []
    pairs = (
        (stick_h, stick), (psi_h, psi), (wz_h, wz), (wy_h, wy), (wx_h, wx), (pot_h, pot),
        (wxb_h, wxb), (wyb_h, wyb), (wzb_h, wzb), (basis_h, basis),
    )
    for k, (source, target) in enumerate(pairs):
        loads.append(pltpu.make_async_copy(source, target, load_sem.at[k]))
    for k in range(3):
        loads[k].start()

    barrier = pltpu.get_barrier_semaphore()
    for dz, dy, dc in STEPS:
        peer = zs[dz] * NYC + ys[dy] * 2 + cores[dc]
        pl.semaphore_signal(barrier, inc=1, device_id=(g, peer), device_id_type=MESH)
    for dx, dy in SECOND:
        peer = myz * NYC + ys[dy] * 2 + mycore
        pl.semaphore_signal(barrier, inc=1, device_id=(groups[dx], peer), device_id_type=MESH)
    for k in (9, 3, 4, 5, 6, 7, 8):
        loads[k].start()

    loads[0].wait()
    col = stick[...]
    fx, cy = frequencies(col)
    fy = jnp.where(cy < 64, cy, cy - NG)
    square = jnp.where(col < 0, 1 << 20, fx * fx + fy * fy).astype(F32)
    lanes = lax.broadcasted_iota(jnp.int32, (NG, NG), 1)
    fz = jnp.where(lanes < 64, lanes, lanes - NG)
    total = jnp.broadcast_to(square, (NG, NG)).T + (fz * fz).astype(F32)
    inside = total <= float(R * R)
    weight[...] = jnp.where(inside, 1.0, 0.0)
    kinetic[...] = jnp.where(inside, total * (2.0 / (R * R)), 0.0)

    def along_z(vectors):
        rows = [triple(jnp.concatenate(parts, axis=1), 1) for parts in vectors]
        return dot(wz[...], jnp.concatenate(rows, axis=0), True)

    loads[1].wait()
    for b in range(NB):
        for c in range(2):
            psi[b, c] = psi[b, c] * weight[...]
    loads[2].wait()
    space = along_z([(psi[b, 0], psi[b, 1]) for b in range(NB)])
    for c in range(2):
        for p in range(2):
            for b in range(NB):
                at = (c * 2 + p) * ND
                send[pl.ds(c * 4 + b * 2 + p, ND, stride=16), :] = space[
                    at : at + ND, b * NG : (b + 1) * NG
                ]

    send[pl.ds(8, ND, stride=16), :] = jnp.broadcast_to(col.astype(F32), (ND, NG))

    pl.semaphore_wait(barrier, ND - 1 + 12)

    def block_at(slot):
        return pl.ds(pl.multiple_of(slot * 8, 8), 8)

    def nine_at(slot):
        return pl.ds(pl.multiple_of(slot * 16, 16), 9)

    def transfer(source, target, place, z, yc, send_sem, recv_sem):
        pltpu.make_async_remote_copy(
            src_ref=source.at[place(yc * NZ + z)], dst_ref=target.at[place(myslot)],
            send_sem=send_sem, recv_sem=recv_sem,
            device_id=(g, z * NYC + yc), device_id_type=MESH,
        ).start()

    for k in (0, 1, 7, 2, 6, 3, 5, 4):
        for dy in (2, 1, 3, 0):
            for dc in range(2):
                if dy + dc + k:
                    yc = ys[dy] * 2 + cores[dc]
                    transfer(send, recv, nine_at, zs[k], yc, fwd_send, fwd_recv.at[myz])
    own = pltpu.make_async_copy(send.at[nine_at(myslot)], recv.at[nine_at(myslot)], own_sem.at[0])
    own.start()

    def products(vectors, trials):
        sums = []
        for v_re, v_im in vectors:
            for c in range(2):
                for b_re, b_im in trials:
                    if c == 0:
                        terms = v_re * b_re + v_im * b_im
                    else:
                        terms = v_im * b_re - v_re * b_im
                    sums.append(jnp.sum(terms, axis=0, keepdims=True))
        return jnp.concatenate(sums, axis=0)

    index = lax.broadcasted_iota(jnp.int32, (2 * NG, NG), 0)
    ramp[0 : 2 * NG, :] = index.astype(F32).astype(BF16)
    ramp[2 * NG : 3 * NG, :] = (index[0:NG] >> 3).astype(F32).astype(BF16)
    loads[9].wait()
    for k in range(NK):
        for c in range(2):
            basis[k, c] = basis[k, c] * weight[...]
    trial[...] = along_z([(basis[k, 0], basis[k, 1]) for k in range(NK)])
    kinetic_part = [
        (kinetic[...] * psi[b, 0], kinetic[...] * psi[b, 1]) for b in range(NB)
    ]
    local[...] = products(kinetic_part, [(basis[k, 0], basis[k, 1]) for k in range(NK)])

    one = jnp.ones((16, NG), BF16)
    zero = jnp.zeros((16, NG), BF16)

    def column(slot):
        return recv[pl.ds(slot * 16 + 8, 1), :].astype(jnp.int32)

    def landed(blocks, sem):
        some = recv.at[pl.ds(0, 9 * blocks)]
        pltpu.make_async_copy(some, some, sem).wait()

    def hot_group(z):
        for q in range(NYC):
            _, lane = packed(column(q * NZ + z))
            lane = jnp.broadcast_to(lane.astype(F32), (16, NG)).astype(BF16)
            at = pl.ds(pl.multiple_of((q * NZ + z) * NG, NG), NG)
            for k in range(16):
                rows = pl.ds(k * 16, 16)
                nhot[rows, at] = jnp.where(ramp[rows, :] == lane, one, zero)

    def place_group(z):
        pieces = []
        for q in range(NZ):
            row, _ = packed(column(q * NZ + z))
            value = recv[pl.ds(pl.multiple_of((q * NZ + z) * 16, 16), 8), :]
            row = jnp.broadcast_to(row.astype(F32), (16, NG)).astype(BF16)
            high, low = split(jnp.concatenate([value, value], axis=0))
            hits = [ramp[pl.ds(2 * NG + k * 16, 16), :] == row for k in range(8)]
            stack = [jnp.where(hit, part, zero) for part in (high, low) for hit in hits]
            pieces.append(jnp.concatenate(stack, axis=0))
        masks = [
            nhot[:, pl.ds(pl.multiple_of((q * NZ + z) * NG, NG), NG)] for q in range(NYC)
        ]
        acc[...] += dot(jnp.concatenate(pieces, axis=1), jnp.concatenate(masks, axis=1), True)

    acc[...] = jnp.zeros_like(acc)
    own.wait()
    landed(NYC - 1, fwd_recv.at[myz])
    hot_group(myz)
    place_group(myz)

    def receive_group(i, carry):
        z = (myz + NZ + ((i + 1) // 2) * (1 - 2 * (i % 2))) % NZ
        landed(NYC, fwd_recv.at[z])
        hot_group(z)
        place_group(z)
        return carry

    lax.fori_loop(1, NYC, receive_group, 0)

    for h in range(2):
        half = slice(h * NG, (h + 1) * NG)
        lref[half, :] = acc[0:NG, half] + acc[NG : 2 * NG, half]
    spot = (lax.broadcasted_iota(jnp.int32, (8, NG), 0) == 0) & (
        lax.broadcasted_iota(jnp.int32, (8, NG), 1) == SPOT
    )
    factor = 1.0 / math.sqrt(NG)
    planes = []
    extra = {}
    for bp in range(4):
        parts = []
        for c in range(2):
            j = c * 4 + bp
            blocks = [lref[pl.ds(h * NG + j, 16, stride=8), :] for h in range(2)]
            first = blocks[0][0:8]
            single = jnp.sum(jnp.where(spot, first, 0.0), axis=1, keepdims=True) * factor
            extra[bp, c] = jnp.broadcast_to(single, (8, NG))
            first = jnp.where(spot, 0.0, first)
            parts.append(jnp.concatenate([first, blocks[0][8:16], blocks[1]], axis=0))
        planes.append(jnp.concatenate(parts, axis=1))
    loads[3].wait()
    along_y = dot(triple(jnp.concatenate(planes, axis=0), 1), wy[...])
    columns = []
    for bp in range(4):
        parts = []
        for c in range(2):
            for t in range(2):
                at = (t * 2 + c) * NG
                parts.append(along_y[bp * 32 : (bp + 1) * 32, at : at + NG])
            parts.append(extra[bp, c])
        columns.append(jnp.concatenate(parts, axis=0))
    high, low = split(jnp.concatenate(columns, axis=1))
    empty = jnp.zeros((512 - 6 * XS, 4 * NG), BF16)
    loads[4].wait()
    field = dot(wx[...], jnp.concatenate([high, low, high, empty], axis=0))
    loads[5].wait()
    both = jnp.concatenate([pot[0], pot[1], pot[0], pot[1]], axis=1)
    product = field * jnp.concatenate([both, both], axis=0)
    loads[6].wait()
    along_x = dot(wxb[...], triple(product, 0))
    planes = []
    for bp in range(4):
        parts = []
        for t in range(2):
            for c in range(2):
                at = c * XS + t * 32
                parts.append(along_x[at : at + 32, bp * NG : (bp + 1) * NG])
        planes.append(jnp.concatenate(parts, axis=1))
    loads[7].wait()
    image = dot(triple(jnp.concatenate(planes, axis=0), 1), wyb[...])
    for bp in range(4):
        for c in range(2):
            j = c * 4 + bp
            at = c * XS + 64
            tail = along_x[at : at + 8, bp * NG : (bp + 1) * NG]
            single = jnp.sum(tail, axis=1, keepdims=True) * factor
            part = image[bp * 32 : (bp + 1) * 32, c * NG : (c + 1) * NG]
            first = jnp.where(spot, single, part[0:8])
            lref[pl.ds(j, 16, stride=8), :] = jnp.concatenate([first, part[8:16]], axis=0)
            lref[pl.ds(NG + j, 16, stride=8), :] = part[16:32]
    high, low = split(jnp.concatenate([lref[0:NG, :], lref[NG : 2 * NG, :]], axis=1))
    acc_left = jnp.concatenate([high, low], axis=0)

    def fetch_group(z):
        for q in range(0, NYC, 2):
            pair = []
            for w in range(2):
                at = pl.ds(pl.multiple_of(((q + w) * NZ + z) * NG, NG), NG)
                pair.append(nhot[:, at])
            found = dot(acc_left, jnp.concatenate(pair, axis=1))
            for w in range(2):
                slot = (q + w) * NZ + z
                row, _ = packed(column(slot))
                here = found[:, w * NG : (w + 1) * NG]
                total = jnp.zeros((8, NG), F32)
                for k in range(16):
                    both = here[k * 8 : k * 8 + 8] + here[NG + k * 8 : NG + k * 8 + 8]
                    total = total + jnp.where(row == k, both, 0.0)
                back[block_at(slot), :] = total

    def return_group(i, carry):
        z = (myz + 4 + ((i + 1) // 2) * (1 - 2 * (i % 2))) % NZ
        fetch_group(z)
        for dy in (2, 1, 3, 0):
            for dc in (1, 0):
                transfer(back, home, block_at, z, ys[dy] * 2 + cores[dc], back_send, back_recv)
        return carry

    lax.fori_loop(0, NZ - 1, return_group, 0)
    fetch_group(myz)
    for dy in (2, 1, 3, 0):
        for dc in (1, 0):
            if dy + dc:
                transfer(back, home, block_at, myz, ys[dy] * 2 + cores[dc], back_send, back_recv)
    own_back = pltpu.make_async_copy(
        back.at[block_at(myslot)], home.at[block_at(myslot)], own_sem.at[1]
    )
    own_back.start()
    loads[8].wait()
    own_back.wait()
    rest = home.at[pl.ds(0, 8 * (ND - 1))]
    pltpu.make_async_copy(rest, rest, back_recv).wait()

    sides = []
    for b in range(NB):
        parts = []
        for c in range(2):
            for p in range(2):
                parts.append(home[pl.ds(c * 4 + b * 2 + p, ND, stride=8), :])
        sides.append(jnp.concatenate(parts, axis=0))
    table = local[...] + products(
        [(side[0:NG], side[NG : 2 * NG]) for side in sides],
        [
            (trial[0:NG, k * NG : (k + 1) * NG], trial[NG : 2 * NG, k * NG : (k + 1) * NG])
            for k in range(NK)
        ],
    )
    table = jnp.sum(table, axis=1, keepdims=True)
    table = table * (1.0 / math.sqrt(4.0 * math.pi * R**3 / 3.0))
    lane = lax.broadcasted_iota(jnp.int32, (1, NG), 1)
    entry = jnp.zeros((1, NG), F32)
    for k in range(16):
        entry = jnp.where(lane == k, table[k : k + 1, :], entry)
    tile1[...] = entry
    pair = pltpu.make_async_remote_copy(
        src_ref=tile1, dst_ref=tile2, send_sem=mar_send.at[0], recv_sem=mar_recv.at[0],
        device_id=(g, myz * NYC + myy * 2 + 1 - mycore), device_id_type=MESH,
    )
    pair.start()
    pair.wait()
    mychip = g * 32 + myz * 4 + myy
    chips[mychip] = entry + tile2[...]

    def tell(dx, z, dy):
        pltpu.make_async_remote_copy(
            src_ref=chips.at[mychip], dst_ref=chips.at[mychip],
            send_sem=mar_send.at[1], recv_sem=mar_recv.at[1],
            device_id=(groups[dx], z * NYC + ys[dy] * 2 + mycore), device_id_type=MESH,
        ).start()

    def tell_far(i, carry):
        z = (myz + 4 + ((i + 1) // 2) * (1 - 2 * (i % 2))) % NZ
        for dx in (2, 1, 3, 0):
            for dy in (2, 1, 3, 0):
                tell(dx, z, dy)
        return carry

    lax.fori_loop(0, NZ - 1, tell_far, 0)
    for dx in (2, 1, 3, 0):
        for dy in (2, 1, 3, 0):
            if dx + dy:
                tell(dx, myz, dy)

    values = dot(wzb[...], triple(jnp.concatenate(sides, axis=1), 0))
    for b in range(NB):
        for c in range(2):
            turned = values[c * NG : (c + 1) * NG, b * NG : (b + 1) * NG].T
            hout[b, c] = weight[...] * turned + kinetic[...] * psi[b, c]

    others = chips.at[pl.ds(0, 127)]
    pltpu.make_async_copy(others, others, mar_recv.at[1]).wait()
    row8 = lax.broadcasted_iota(jnp.int32, (8, NG), 0)
    lane8 = lax.broadcasted_iota(jnp.int32, (8, NG), 1)
    final = jnp.zeros((8, NG), F32)
    for group in range(4):
        parts = [chips[group * 32 + k] for k in range(32)]
        while len(parts) > 1:
            parts = [parts[k] + parts[k + 1] for k in range(0, len(parts), 2)]
        total = parts[0]
        for b in range(NB):
            picked = jnp.where(lane8 == row8 + b * 8, total, 0.0)
            picked = jnp.sum(picked, axis=1, keepdims=True)
            final = jnp.where(lane8 == group * NB + b, picked, final)
    margin[0] = final[0:NK, 0 : 4 * NB]
    margin[1] = final[NK : 2 * NK, 0 : 4 * NB]

    sent = recv.at[pl.ds(0, 9 * (ND - 1))]
    pltpu.make_async_copy(sent, sent, fwd_send).wait()
    pltpu.make_async_copy(rest, rest, back_send).wait()
    pltpu.make_async_copy(others, others, mar_send.at[1]).wait()


def body(psi, potential, basis, stick_map):
    shapes = [
        (psi.shape, F32), (potential.shape, F32), (basis.shape, F32), ((1, NG), jnp.int32),
    ]
    scratch = [pltpu.VMEM(shape, kind) for shape, kind in shapes]
    scratch += [pltpu.VMEM(table.shape, BF16) for table in TABLES]
    scratch += [
        pltpu.VMEM((NG, NG), F32),
        pltpu.VMEM((NG, NG), F32),
        pltpu.VMEM((ND * 16, NG), F32),
        pltpu.VMEM((ND * 16, NG), F32),
        pltpu.VMEM((ND * 8, NG), F32),
        pltpu.VMEM((ND * 8, NG), F32),
        pltpu.VMEM((2 * NG, ND * NG), BF16),
        pltpu.VMEM((2 * NG, 2 * NG), F32),
        pltpu.VMEM((2 * NG, NG), F32),
        pltpu.VMEM((2 * NG, NK * NG), F32),
        pltpu.VMEM((16, NG), F32),
        pltpu.VMEM((3 * NG, NG), BF16),
        pltpu.VMEM((1, NG), F32),
        pltpu.VMEM((1, NG), F32),
        pltpu.VMEM((128, 1, NG), F32),
        pltpu.SemaphoreType.DMA((10,)),
        pltpu.SemaphoreType.DMA((2,)),
        pltpu.SemaphoreType.DMA,
        pltpu.SemaphoreType.DMA((NYC,)),
        pltpu.SemaphoreType.DMA,
        pltpu.SemaphoreType.DMA,
        pltpu.SemaphoreType.DMA((2,)),
        pltpu.SemaphoreType.DMA((2,)),
    ]
    hpsi, margin = pl.pallas_call(
        kernel,
        out_shape=(
            pltpu.VMEM(psi.shape, F32),
            pltpu.VMEM((2, NK, 4 * NB), F32),
        ),
        in_specs=[pl.BlockSpec(memory_space=pltpu.HBM)] * (4 + len(TABLES)),
        out_specs=(
            pl.BlockSpec(memory_space=pltpu.VMEM),
            pl.BlockSpec(memory_space=pltpu.VMEM),
        ),
        scratch_shapes=scratch,
        compiler_params=pltpu.CompilerParams(
            collective_id=0, has_side_effects=True, vmem_limit_bytes=VMEM_BYTES
        ),
        cost_estimate=pl.CostEstimate(
            flops=20_000_000_000, bytes_accessed=6_000_000, transcendentals=0
        ),
    )(psi, potential, basis, stick_map.reshape(1, NG), *[jnp.asarray(t) for t in TABLES])
    return hpsi, margin.transpose(0, 2, 1)


def solution(mesh):
    placed = (
        P("bgrp", None, "fft", None),
        P("fft", None, None),
        P(None, None, "fft", None),
        P("fft"),
    )
    return jax.shard_map(
        body,
        mesh=mesh,
        in_specs=placed,
        out_specs=(P("bgrp", None, "fft", None), P()),
        check_vma=False,
    )
```

```python
import functools
import math

import jax
import jax.numpy as jnp
import ml_dtypes
import numpy as np
from jax import lax
from jax.experimental import pallas as pl
from jax.experimental.pallas import tpu as pltpu
from jax.sharding import PartitionSpec as P

NG = 128
R = 32
NB = 2
NK = 4
ND = 64
NZ = 8
NYC = 8
XS = 72
SPOT = 80
VMEM_BYTES = 62 * 1024 * 1024
F32 = jnp.float32
BF16 = jnp.bfloat16
MESH = pl.DeviceIdType.MESH


def split_np(table):
    high = table.astype(np.float32).astype(ml_dtypes.bfloat16)
    low = (table - high.astype(np.float64)).astype(np.float32).astype(ml_dtypes.bfloat16)
    return high, low


def phases(rows, cols):
    angle = 2.0 * np.pi / NG * (np.outer(rows, cols) % NG)
    return np.cos(angle) / math.sqrt(NG), np.sin(angle) / math.sqrt(NG)


def build_tables():
    index = np.arange(NG)
    slot = np.arange(ND)
    device = (slot % NZ) * NYC + slot // NZ
    z_rows = np.concatenate([2 * device, 2 * device + 1])
    cos, sin = phases(z_rows, index)
    wz = np.block([[cos, -sin], [sin, cos]])
    blocks = []
    for shifted in (0, 1):
        freq = index - 64 if shifted else index
        inner = (index >= 33) & (index <= 95)
        used = inner if shifted else ~inner
        cos, sin = phases(freq, index)
        cos, sin = cos * used[:, None], sin * used[:, None]
        blocks.append(np.block([[cos, sin], [-sin, cos]]))
    wy = np.concatenate(blocks, axis=1)
    freq = np.zeros(XS)
    freq[:32] = np.arange(32)
    freq[32:64] = -np.arange(32)
    freq[32] = -R
    freq[64] = R
    cos, sin = phases(index, freq)
    cos[:, 65:] = 0.0
    sin[:, 65:] = 0.0
    wx = np.block([[cos, -sin], [sin, cos]])
    tables = []
    for table, side in ((wz, 1), (wy, 0), (wx, 1), (wx.T, 1), (wy.T, 0), (wz.T, 1)):
        high, low = split_np(table)
        tables.append(np.concatenate([high, high, low], axis=side))
    pad = np.zeros((2 * NG, 512 - 6 * XS), ml_dtypes.bfloat16)
    tables[2] = np.concatenate([tables[2], pad], axis=1)
    return tables


TABLES = build_tables()


def hops(dz, dy, dc):
    return min(dz, NZ - dz) + min(dy, 4 - dy) + 0.3 * dc


STEPS = sorted(
    ((dz, dy, dc) for dz in range(NZ) for dy in range(4) for dc in range(2)),
    key=lambda step: -hops(*step),
)[:-1]
SECOND = [(dx, dy) for dx in (2, 1, 3) for dy in (2, 1, 3, 0)]
FAR_Z = (4, 3, 5, 2, 6, 1, 7, 0)


def split(value):
    high = value.astype(BF16)
    low = (value - high.astype(F32)).astype(BF16)
    return high, low


def dot(left, right, transposed=False):
    dims = (((1,), (1 if transposed else 0,)), ((), ()))
    return lax.dot_general(left, right, dims, preferred_element_type=F32)


def triple(value, axis):
    high, low = split(value)
    return jnp.concatenate([high, low, high], axis=axis)


def frequencies(col):
    cx = col >> 7
    cy = col & 127
    fx = jnp.where(cx < 64, cx, cx - NG)
    return fx, cy


def packed(col):
    fx, cy = frequencies(col)
    row = jnp.abs(fx) & 31
    lane = jnp.where(fx < 0, (cy + 64) & 127, cy)
    lane = jnp.where(fx == R, SPOT, lane)
    lane = lane + (row >> 4) * NG
    row = jnp.where(col < 0, -1, row & 15)
    return row, lane


def kernel(
    psi_h, pot_h, basis_h, stick_h, wz_h, wy_h, wx_h, wxb_h, wyb_h, wzb_h,
    hout, margin,
    psi, pot, basis, stick, wz, wy, wx, wxb, wyb, wzb,
    weight, kinetic, send, recv, back, home, nhot, acc, lref, trial, local, ramp,
    tile1, tile2, chips,
    load_sem, own_sem, fwd_send, fwd_recv,
    back_send, back_recv, mar_send, mar_recv,
):
    g = lax.axis_index("bgrp")
    me = lax.axis_index("fft")
    myz = me // NYC
    myyc = me % NYC
    myy = myyc // 2
    mycore = myyc % 2
    myslot = myyc * NZ + myz

    zs = [(myz + k) % NZ for k in range(NZ)]
    ys = [(myy + k) % 4 for k in range(4)]
    cores = [mycore, 1 - mycore]
    groups = [(g + k) % 4 for k in range(4)]

    loads = []
    pairs = (
        (stick_h, stick), (psi_h, psi), (wz_h, wz), (wy_h, wy), (wx_h, wx), (pot_h, pot),
        (wxb_h, wxb), (wyb_h, wyb), (wzb_h, wzb), (basis_h, basis),
    )
    for k, (source, target) in enumerate(pairs):
        loads.append(pltpu.make_async_copy(source, target, load_sem.at[k]))
    for k in range(3):
        loads[k].start()

    barrier = pltpu.get_barrier_semaphore()
    for dz, dy, dc in STEPS:
        peer = zs[dz] * NYC + ys[dy] * 2 + cores[dc]
        pl.semaphore_signal(barrier, inc=1, device_id=(g, peer), device_id_type=MESH)
    for dx, dy in SECOND:
        peer = myz * NYC + ys[dy] * 2 + mycore
        pl.semaphore_signal(barrier, inc=1, device_id=(groups[dx], peer), device_id_type=MESH)
    for k in (9, 3, 4, 5, 6, 7, 8):
        loads[k].start()

    loads[0].wait()
    col = stick[...]
    fx, cy = frequencies(col)
    fy = jnp.where(cy < 64, cy, cy - NG)
    square = jnp.where(col < 0, 1 << 20, fx * fx + fy * fy).astype(F32)
    lanes = lax.broadcasted_iota(jnp.int32, (NG, NG), 1)
    fz = jnp.where(lanes < 64, lanes, lanes - NG)
    total = jnp.broadcast_to(square, (NG, NG)).T + (fz * fz).astype(F32)
    inside = total <= float(R * R)
    weight[...] = jnp.where(inside, 1.0, 0.0)
    kinetic[...] = jnp.where(inside, total * (2.0 / (R * R)), 0.0)

    def along_z(vectors):
        rows = [triple(jnp.concatenate(parts, axis=1), 1) for parts in vectors]
        return dot(wz[...], jnp.concatenate(rows, axis=0), True)

    loads[1].wait()
    for b in range(NB):
        for c in range(2):
            psi[b, c] = psi[b, c] * weight[...]
    loads[2].wait()
    space = along_z([(psi[b, 0], psi[b, 1]) for b in range(NB)])
    for c in range(2):
        for p in range(2):
            for b in range(NB):
                at = (c * 2 + p) * ND
                send[pl.ds(c * 4 + b * 2 + p, ND, stride=16), :] = space[
                    at : at + ND, b * NG : (b + 1) * NG
                ]

    send[pl.ds(8, ND, stride=16), :] = jnp.broadcast_to(col.astype(F32), (ND, NG))

    pl.semaphore_wait(barrier, ND - 1 + 12)

    def block_at(slot):
        return pl.ds(pl.multiple_of(slot * 8, 8), 8)

    def nine_at(slot):
        return pl.ds(pl.multiple_of(slot * 16, 16), 9)

    def transfer(source, target, place, z, yc, send_sem, recv_sem):
        pltpu.make_async_remote_copy(
            src_ref=source.at[place(yc * NZ + z)], dst_ref=target.at[place(myslot)],
            send_sem=send_sem, recv_sem=recv_sem,
            device_id=(g, z * NYC + yc), device_id_type=MESH,
        ).start()

    for k in (0, 1, 7, 2, 6, 3, 5, 4):
        for dy in (2, 1, 3, 0):
            for dc in range(2):
                if dy + dc + k:
                    yc = ys[dy] * 2 + cores[dc]
                    transfer(send, recv, nine_at, zs[k], yc, fwd_send, fwd_recv.at[myz])
    own = pltpu.make_async_copy(send.at[nine_at(myslot)], recv.at[nine_at(myslot)], own_sem.at[0])
    own.start()

    def products(vectors, trials):
        sums = []
        for v_re, v_im in vectors:
            for c in range(2):
                for b_re, b_im in trials:
                    if c == 0:
                        terms = v_re * b_re + v_im * b_im
                    else:
                        terms = v_im * b_re - v_re * b_im
                    sums.append(jnp.sum(terms, axis=0, keepdims=True))
        return jnp.concatenate(sums, axis=0)

    index = lax.broadcasted_iota(jnp.int32, (2 * NG, NG), 0)
    ramp[0 : 2 * NG, :] = index.astype(F32).astype(BF16)
    ramp[2 * NG : 3 * NG, :] = (index[0:NG] >> 3).astype(F32).astype(BF16)
    loads[9].wait()
    for k in range(NK):
        for c in range(2):
            basis[k, c] = basis[k, c] * weight[...]
    trial[...] = along_z([(basis[k, 0], basis[k, 1]) for k in range(NK)])
    kinetic_part = [
        (kinetic[...] * psi[b, 0], kinetic[...] * psi[b, 1]) for b in range(NB)
    ]
    local[...] = products(kinetic_part, [(basis[k, 0], basis[k, 1]) for k in range(NK)])

    one = jnp.ones((16, NG), BF16)
    zero = jnp.zeros((16, NG), BF16)

    def column(slot):
        return recv[pl.ds(slot * 16 + 8, 1), :].astype(jnp.int32)

    def landed(blocks, sem):
        some = recv.at[pl.ds(0, 9 * blocks)]
        pltpu.make_async_copy(some, some, sem).wait()

    def hot_group(z):
        for q in range(NYC):
            _, lane = packed(column(q * NZ + z))
            lane = jnp.broadcast_to(lane.astype(F32), (16, NG)).astype(BF16)
            at = pl.ds(pl.multiple_of((q * NZ + z) * NG, NG), NG)
            for k in range(16):
                rows = pl.ds(k * 16, 16)
                nhot[rows, at] = jnp.where(ramp[rows, :] == lane, one, zero)

    def place_group(z):
        pieces = []
        for q in range(NZ):
            row, _ = packed(column(q * NZ + z))
            value = recv[pl.ds(pl.multiple_of((q * NZ + z) * 16, 16), 8), :]
            row = jnp.broadcast_to(row.astype(F32), (16, NG)).astype(BF16)
            high, low = split(jnp.concatenate([value, value], axis=0))
            hits = [ramp[pl.ds(2 * NG + k * 16, 16), :] == row for k in range(8)]
            stack = [jnp.where(hit, part, zero) for part in (high, low) for hit in hits]
            pieces.append(jnp.concatenate(stack, axis=0))
        masks = [
            nhot[:, pl.ds(pl.multiple_of((q * NZ + z) * NG, NG), NG)] for q in range(NYC)
        ]
        acc[...] += dot(jnp.concatenate(pieces, axis=1), jnp.concatenate(masks, axis=1), True)

    acc[...] = jnp.zeros_like(acc)
    own.wait()
    landed(NYC - 1, fwd_recv.at[myz])
    hot_group(myz)
    place_group(myz)

    def receive_group(i, carry):
        z = (myz + NZ + ((i + 1) // 2) * (1 - 2 * (i % 2))) % NZ
        landed(NYC, fwd_recv.at[z])
        hot_group(z)
        place_group(z)
        return carry

    lax.fori_loop(1, NYC, receive_group, 0)

    for h in range(2):
        half = slice(h * NG, (h + 1) * NG)
        lref[half, :] = acc[0:NG, half] + acc[NG : 2 * NG, half]
    spot = (lax.broadcasted_iota(jnp.int32, (8, NG), 0) == 0) & (
        lax.broadcasted_iota(jnp.int32, (8, NG), 1) == SPOT
    )
    factor = 1.0 / math.sqrt(NG)
    planes = []
    extra = {}
    for bp in range(4):
        parts = []
        for c in range(2):
            j = c * 4 + bp
            blocks = [lref[pl.ds(h * NG + j, 16, stride=8), :] for h in range(2)]
            first = blocks[0][0:8]
            single = jnp.sum(jnp.where(spot, first, 0.0), axis=1, keepdims=True) * factor
            extra[bp, c] = jnp.broadcast_to(single, (8, NG))
            first = jnp.where(spot, 0.0, first)
            parts.append(jnp.concatenate([first, blocks[0][8:16], blocks[1]], axis=0))
        planes.append(jnp.concatenate(parts, axis=1))
    loads[3].wait()
    along_y = dot(triple(jnp.concatenate(planes, axis=0), 1), wy[...])
    columns = []
    for bp in range(4):
        parts = []
        for c in range(2):
            for t in range(2):
                at = (t * 2 + c) * NG
                parts.append(along_y[bp * 32 : (bp + 1) * 32, at : at + NG])
            parts.append(extra[bp, c])
        columns.append(jnp.concatenate(parts, axis=0))
    high, low = split(jnp.concatenate(columns, axis=1))
    empty = jnp.zeros((512 - 6 * XS, 4 * NG), BF16)
    loads[4].wait()
    field = dot(wx[...], jnp.concatenate([high, low, high, empty], axis=0))
    loads[5].wait()
    both = jnp.concatenate([pot[0], pot[1], pot[0], pot[1]], axis=1)
    product = field * jnp.concatenate([both, both], axis=0)
    loads[6].wait()
    along_x = dot(wxb[...], triple(product, 0))
    planes = []
    for bp in range(4):
        parts = []
        for t in range(2):
            for c in range(2):
                at = c * XS + t * 32
                parts.append(along_x[at : at + 32, bp * NG : (bp + 1) * NG])
        planes.append(jnp.concatenate(parts, axis=1))
    loads[7].wait()
    image = dot(triple(jnp.concatenate(planes, axis=0), 1), wyb[...])
    for bp in range(4):
        for c in range(2):
            j = c * 4 + bp
            at = c * XS + 64
            tail = along_x[at : at + 8, bp * NG : (bp + 1) * NG]
            single = jnp.sum(tail, axis=1, keepdims=True) * factor
            part = image[bp * 32 : (bp + 1) * 32, c * NG : (c + 1) * NG]
            first = jnp.where(spot, single, part[0:8])
            lref[pl.ds(j, 16, stride=8), :] = jnp.concatenate([first, part[8:16]], axis=0)
            lref[pl.ds(NG + j, 16, stride=8), :] = part[16:32]
    high, low = split(jnp.concatenate([lref[0:NG, :], lref[NG : 2 * NG, :]], axis=1))
    acc_left = jnp.concatenate([high, low], axis=1)

    def fetch_group(z):
        for q in range(0, NYC, 2):
            pair = []
            for w in range(2):
                at = pl.ds(pl.multiple_of(((q + w) * NZ + z) * NG, NG), NG)
                pair.append(nhot[:, at])
            masks = jnp.concatenate(pair, axis=1)
            found = dot(acc_left, jnp.concatenate([masks, masks], axis=0))
            for w in range(2):
                slot = (q + w) * NZ + z
                row, _ = packed(column(slot))
                here = found[:, w * NG : (w + 1) * NG]
                total = jnp.zeros((8, NG), F32)
                for k in range(16):
                    total = total + jnp.where(row == k, here[k * 8 : k * 8 + 8], 0.0)
                back[block_at(slot), :] = total

    def return_group(i, carry):
        z = (myz + 4 + ((i + 1) // 2) * (1 - 2 * (i % 2))) % NZ
        fetch_group(z)
        for dy in (2, 1, 3, 0):
            for dc in (1, 0):
                transfer(back, home, block_at, z, ys[dy] * 2 + cores[dc], back_send, back_recv)
        return carry

    lax.fori_loop(0, NZ - 1, return_group, 0)
    fetch_group(myz)
    for dy in (2, 1, 3, 0):
        for dc in (1, 0):
            if dy + dc:
                transfer(back, home, block_at, myz, ys[dy] * 2 + cores[dc], back_send, back_recv)
    own_back = pltpu.make_async_copy(
        back.at[block_at(myslot)], home.at[block_at(myslot)], own_sem.at[1]
    )
    own_back.start()
    loads[8].wait()
    own_back.wait()
    rest = home.at[pl.ds(0, 8 * (ND - 1))]
    pltpu.make_async_copy(rest, rest, back_recv).wait()

    sides = []
    for b in range(NB):
        parts = []
        for c in range(2):
            for p in range(2):
                parts.append(home[pl.ds(c * 4 + b * 2 + p, ND, stride=8), :])
        sides.append(jnp.concatenate(parts, axis=0))
    table = local[...] + products(
        [(side[0:NG], side[NG : 2 * NG]) for side in sides],
        [
            (trial[0:NG, k * NG : (k + 1) * NG], trial[NG : 2 * NG, k * NG : (k + 1) * NG])
            for k in range(NK)
        ],
    )
    table = jnp.sum(table, axis=1, keepdims=True)
    table = table * (1.0 / math.sqrt(4.0 * math.pi * R**3 / 3.0))
    lane = lax.broadcasted_iota(jnp.int32, (1, NG), 1)
    entry = jnp.zeros((1, NG), F32)
    for k in range(16):
        entry = jnp.where(lane == k, table[k : k + 1, :], entry)
    tile1[...] = entry
    pair = pltpu.make_async_remote_copy(
        src_ref=tile1, dst_ref=tile2, send_sem=mar_send.at[0], recv_sem=mar_recv.at[0],
        device_id=(g, myz * NYC + myy * 2 + 1 - mycore), device_id_type=MESH,
    )
    pair.start()
    pair.wait()
    mychip = g * 32 + myz * 4 + myy
    chips[mychip] = entry + tile2[...]

    def tell(dx, z, dy):
        pltpu.make_async_remote_copy(
            src_ref=chips.at[mychip], dst_ref=chips.at[mychip],
            send_sem=mar_send.at[1], recv_sem=mar_recv.at[1],
            device_id=(groups[dx], z * NYC + ys[dy] * 2 + mycore), device_id_type=MESH,
        ).start()

    def tell_far(i, carry):
        z = (myz + 4 + ((i + 1) // 2) * (1 - 2 * (i % 2))) % NZ
        for dx in (2, 1, 3, 0):
            for dy in (2, 1, 3, 0):
                tell(dx, z, dy)
        return carry

    lax.fori_loop(0, NZ - 1, tell_far, 0)
    for dx in (2, 1, 3, 0):
        for dy in (2, 1, 3, 0):
            if dx + dy:
                tell(dx, myz, dy)

    values = dot(wzb[...], triple(jnp.concatenate(sides, axis=1), 0))
    for b in range(NB):
        for c in range(2):
            turned = values[c * NG : (c + 1) * NG, b * NG : (b + 1) * NG].T
            hout[b, c] = weight[...] * turned + kinetic[...] * psi[b, c]

    others = chips.at[pl.ds(0, 127)]
    pltpu.make_async_copy(others, others, mar_recv.at[1]).wait()
    row8 = lax.broadcasted_iota(jnp.int32, (8, NG), 0)
    lane8 = lax.broadcasted_iota(jnp.int32, (8, NG), 1)
    final = jnp.zeros((8, NG), F32)
    for group in range(4):
        parts = [chips[group * 32 + k] for k in range(32)]
        while len(parts) > 1:
            parts = [parts[k] + parts[k + 1] for k in range(0, len(parts), 2)]
        total = parts[0]
        for b in range(NB):
            picked = jnp.where(lane8 == row8 + b * 8, total, 0.0)
            picked = jnp.sum(picked, axis=1, keepdims=True)
            final = jnp.where(lane8 == group * NB + b, picked, final)
    margin[0] = final[0:NK, 0 : 4 * NB]
    margin[1] = final[NK : 2 * NK, 0 : 4 * NB]

    sent = recv.at[pl.ds(0, 9 * (ND - 1))]
    pltpu.make_async_copy(sent, sent, fwd_send).wait()
    pltpu.make_async_copy(rest, rest, back_send).wait()
    pltpu.make_async_copy(others, others, mar_send.at[1]).wait()


def body(psi, potential, basis, stick_map):
    shapes = [
        (psi.shape, F32), (potential.shape, F32), (basis.shape, F32), ((1, NG), jnp.int32),
    ]
    scratch = [pltpu.VMEM(shape, kind) for shape, kind in shapes]
    scratch += [pltpu.VMEM(table.shape, BF16) for table in TABLES]
    scratch += [
        pltpu.VMEM((NG, NG), F32),
        pltpu.VMEM((NG, NG), F32),
        pltpu.VMEM((ND * 16, NG), F32),
        pltpu.VMEM((ND * 16, NG), F32),
        pltpu.VMEM((ND * 8, NG), F32),
        pltpu.VMEM((ND * 8, NG), F32),
        pltpu.VMEM((2 * NG, ND * NG), BF16),
        pltpu.VMEM((2 * NG, 2 * NG), F32),
        pltpu.VMEM((2 * NG, NG), F32),
        pltpu.VMEM((2 * NG, NK * NG), F32),
        pltpu.VMEM((16, NG), F32),
        pltpu.VMEM((3 * NG, NG), BF16),
        pltpu.VMEM((1, NG), F32),
        pltpu.VMEM((1, NG), F32),
        pltpu.VMEM((128, 1, NG), F32),
        pltpu.SemaphoreType.DMA((10,)),
        pltpu.SemaphoreType.DMA((2,)),
        pltpu.SemaphoreType.DMA,
        pltpu.SemaphoreType.DMA((NYC,)),
        pltpu.SemaphoreType.DMA,
        pltpu.SemaphoreType.DMA,
        pltpu.SemaphoreType.DMA((2,)),
        pltpu.SemaphoreType.DMA((2,)),
    ]
    hpsi, margin = pl.pallas_call(
        kernel,
        out_shape=(
            pltpu.VMEM(psi.shape, F32),
            pltpu.VMEM((2, NK, 4 * NB), F32),
        ),
        in_specs=[pl.BlockSpec(memory_space=pltpu.HBM)] * (4 + len(TABLES)),
        out_specs=(
            pl.BlockSpec(memory_space=pltpu.VMEM),
            pl.BlockSpec(memory_space=pltpu.VMEM),
        ),
        scratch_shapes=scratch,
        compiler_params=pltpu.CompilerParams(
            collective_id=0, has_side_effects=True, vmem_limit_bytes=VMEM_BYTES
        ),
        cost_estimate=pl.CostEstimate(
            flops=20_000_000_000, bytes_accessed=6_000_000, transcendentals=0
        ),
    )(psi, potential, basis, stick_map.reshape(1, NG), *[jnp.asarray(t) for t in TABLES])
    return hpsi, margin.transpose(0, 2, 1)


def solution(mesh):
    placed = (
        P("bgrp", None, "fft", None),
        P("fft", None, None),
        P(None, None, "fft", None),
        P("fft"),
    )
    return jax.shard_map(
        body,
        mesh=mesh,
        in_specs=placed,
        out_specs=(P("bgrp", None, "fft", None), P()),
        check_vma=False,
    )
```
